128 devices in a mesh: ctx: 64 (over y_lo, x, z, core), dp: 2 (over y_hi).
Axes of the slice: x: 4, y: 4 (y_hi: 2, y_lo: 2; y = y_hi * 2 + y_lo), z: 4, core: 2. Of those that a mesh axis runs over, the one named last changes fastest.
Arguments:
- query_proj: bfloat16 [2, 8192, 1024], P('dp', 'ctx'), may hold values from -6 to 6
- key_proj: bfloat16 [2, 8192, 1024], P('dp', 'ctx'), may hold values from -6 to 6
- value_proj: bfloat16 [2, 8192, 1024], P('dp', 'ctx'), may hold values from -6 to 6
- grad_out: bfloat16 [2, 8192, 4096], P('dp', 'ctx'), may hold values from -6 to 6
- out_weight: bfloat16 [1024, 4096], P('ctx'), may hold values from -0.1875 to 0.1875
- short_taps: float32 [3, 1024, 7], replicated, may hold values from -2 to 2
- residues: float32 [1024, 16], replicated, may hold values from -1.5 to 1.5
- decay_rate: float32 [1024, 16], replicated, may hold values from 3.0517578e-05 to 0.05
Outputs:
- grad_query: bfloat16 [2, 8192, 1024], P('dp', 'ctx')
- grad_key: bfloat16 [2, 8192, 1024], P('dp', 'ctx')
- grad_value: bfloat16 [2, 8192, 1024], P('dp', 'ctx')
- weight_grad: float32 [1024, 4096], P('ctx')
- taps_grad: float32 [3, 1024, 7], replicated
- residue_grad: float32 [1024, 16], replicated
The draws below stay inside these ranges and needn't reach their ends.
All inputs are finite; a program needn't handle non-finite values.
Results may differ from the reference program's by a relative error of at most 0.0075.
Values may be sent and summed in bfloat16 or wider, within the bound.
No kernel may reach another device: no remote copies, remote signals or barrier semaphores. Data moves between devices by JAX's collectives and lax.ppermute only.
A program may use at most 192 MiB of HBM per device.

```python
import math
import jax
import jax.numpy as jnp
from jax import lax

C = 1024
D = 4096
M = 16
L = 8192
BATCH = 2


def level_of(stream_key, extent, cuts, smallest, largest):
    def one(position, parts):
        heights = jax.random.uniform(jax.random.fold_in(jax.random.fold_in(stream_key, 6), position), (parts,), jnp.float32, smallest / len(cuts), largest / len(cuts))
        return jnp.repeat(jnp.exp(heights), extent[position] // parts).reshape((-1,) + (1,) * (len(extent) - position - 1))

    level = one(*cuts[0])
    for cut in cuts[1:]:
        level = level * one(*cut)
    return level


def noise(own_key, shape, spread, reach, pieces=(), dtype=jnp.bfloat16):
    values = jax.random.normal(own_key, shape, jnp.float32) * spread
    if len(pieces) > 0:
        values = level_of(own_key, shape, pieces, -0.22, 0.18) * values
    return jnp.clip(values, min=-reach, max=reach).astype(dtype)


def setup_inputs(seed: int = 0) -> dict:
    arg_keys = jax.random.split(jax.random.key(seed), 9)
    return {
        "query_proj": noise(arg_keys[0], (BATCH, L, C), 1.0, 6.0, ((0, 2), (1, 64))),
        "key_proj": noise(arg_keys[1], (BATCH, L, C), 1.0, 6.0, ((0, 2), (1, 64))),
        "value_proj": noise(arg_keys[2], (BATCH, L, C), 1.0, 6.0, ((0, 2), (1, 64))),
        "grad_out": noise(arg_keys[3], (BATCH, L, D), 1.0, 6.0, ((0, 2), (1, 64))),
        "out_weight": noise(arg_keys[4], (C, D), C ** -0.5, 0.1875, ((0, 64),)),
        "short_taps": noise(arg_keys[5], (3, C, 7), 7 ** -0.5, 2.0, (), jnp.float32),
        "residues": noise(arg_keys[6], (C, M), M ** -0.5, 1.5, (), jnp.float32),
        "decay_rate": jnp.clip(jnp.exp(jax.random.uniform(arg_keys[7], (C, M), jnp.float32, math.log(3.0517578125e-05), math.log(0.05))), 3.0517578125e-05, 0.05),
    }


def shift_sum(field, taps):
    length = field.shape[1]
    padded = jnp.pad(field, ((0, 0), (6, 0), (0, 0)))
    result = jnp.zeros_like(field)
    for lag in range(7):
        result = result + taps[:, lag] * padded[:, 6 - lag:6 - lag + length, :]
    return result

def adjoint_sum(grad, taps):
    length = grad.shape[1]
    padded = jnp.pad(grad, ((0, 0), (0, 6), (0, 0)))
    result = jnp.zeros_like(grad)
    for lag in range(7):
        result = result + taps[:, lag] * padded[:, lag:lag + length, :]
    return result

def tap_terms(grad, field):
    length = field.shape[1]
    padded = jnp.pad(field, ((0, 0), (6, 0), (0, 0)))
    return jnp.stack([lax.optimization_barrier(jnp.sum(grad * padded[:, 6 - lag:6 - lag + length, :], axis=(0, 1))) for lag in range(7)], axis=-1)

def reference(query_proj, key_proj, value_proj, grad_out, out_weight, short_taps, residues, decay_rate):
    query_f = query_proj.astype(jnp.float32)
    key_f = key_proj.astype(jnp.float32)
    value_f = value_proj.astype(jnp.float32)
    shaped_q = shift_sum(query_f, short_taps[0])
    shaped_k = shift_sum(key_f, short_taps[1])
    shaped_v = shift_sum(value_f, short_taps[2])
    mixed = shaped_k * shaped_v
    factor = jnp.exp(-decay_rate)
    norm = jnp.sqrt(-jnp.expm1(-2.0 * decay_rate))
    coef = residues * norm
    start = jnp.zeros((BATCH, C, M), jnp.float32)

    def forward_step(state, column):
        state = factor * state + column[:, :, None]
        return (state, lax.optimization_barrier(jnp.sum(coef * state, axis=-1)))
    _, filtered = lax.scan(forward_step, start, jnp.swapaxes(mixed, 0, 1))
    filtered = jnp.swapaxes(filtered, 0, 1)
    flat_out = grad_out.reshape(-1, D)
    upstream = jnp.dot(flat_out, out_weight.T, preferred_element_type=jnp.float32).reshape(BATCH, -1, C)
    gated = (shaped_q * filtered).astype(jnp.bfloat16)
    weight_grad = jnp.dot(gated.reshape(-1, C).T, flat_out, preferred_element_type=jnp.float32)
    grad_filtered = upstream * shaped_q
    grad_qs = upstream * filtered

    def backward_step(carry, columns):
        adjoint, total = carry
        grad_col, mix_col = columns
        adjoint = factor * adjoint + grad_col[:, :, None]
        total = total + mix_col[:, :, None] * adjoint
        return ((adjoint, total), lax.optimization_barrier(jnp.sum(coef * adjoint, axis=-1)))
    (_, total), grad_mixed = lax.scan(backward_step, (start, start), (jnp.swapaxes(grad_filtered, 0, 1), jnp.swapaxes(mixed, 0, 1)), reverse=True)
    grad_mixed = jnp.swapaxes(grad_mixed, 0, 1)
    residue_grad = norm * lax.optimization_barrier(jnp.sum(total, axis=0))
    grad_ks = grad_mixed * shaped_v
    grad_vs = grad_mixed * shaped_k
    grad_query = adjoint_sum(grad_qs, short_taps[0]).astype(jnp.bfloat16)
    grad_key = adjoint_sum(grad_ks, short_taps[1]).astype(jnp.bfloat16)
    grad_value = adjoint_sum(grad_vs, short_taps[2]).astype(jnp.bfloat16)
    taps_grad = jnp.stack([tap_terms(grad_qs, query_f), tap_terms(grad_ks, key_f), tap_terms(grad_vs, value_f)])
    return (grad_query, grad_key, grad_value, weight_grad, taps_grad, residue_grad)
```

```python
import functools

import jax
import jax.numpy as jnp
from jax import lax
from jax.experimental import pallas as pl
from jax.experimental.pallas import tpu as pltpu
from jax.sharding import Mesh, PartitionSpec as P

BF = jnp.bfloat16
F32 = jnp.float32
T = 128
C = 1024
D = 4096
M = 16
PAD = 64
ROWS = 8 * T
XR = PAD + ROWS
CTX = ("yl", "x", "z", "core")
GRP = ("yl", "x", "z")
LEVELS = (("core", 2, 1), ("z", 4, 2), ("x", 4, 8), ("yl", 2, 32))

VMEM = pl.BlockSpec(memory_space=pltpu.VMEM)


def call(body, outs, ins, scratch=(), flops=10_000_000):
    return pl.pallas_call(
        body,
        out_shape=outs,
        in_specs=[VMEM] * len(ins),
        out_specs=[VMEM] * len(outs),
        scratch_shapes=list(scratch),
        compiler_params=pltpu.CompilerParams(vmem_limit_bytes=40 * 1024 * 1024),
        cost_estimate=pl.CostEstimate(flops=flops, bytes_accessed=4_000_000, transcendentals=0),
    )(*ins)


def row(ref, at):
    return ref[pl.ds(pl.multiple_of(at, 8), 8), :]


def put(ref, at, value):
    ref[pl.ds(pl.multiple_of(at, 8), 8), :] = value


def shape_kernel(q, k, v, halo, taps, factor, xs, ys, ends):
    for i, src in enumerate((q, k, v)):
        base = i * XR
        xs[base : base + PAD, :] = halo[i * PAD : (i + 1) * PAD, :]
        for g in range(T // 16):
            for s in range(8):
                val = src[16 * g : 16 * g + 16, 128 * s : 128 * s + 128].astype(F32)
                xs[pl.ds(base + PAD + 128 * g + s, 16, stride=8), :] = val
    for i in range(3):
        tap = [taps[(i * 7 + j) * 8 : (i * 7 + j) * 8 + 8, :] for j in range(7)]

        def body(b, _):
            at = i * XR + PAD + b * 64
            win = [row(xs, at + 8 * d) for d in range(-6, 8)]
            for t in range(8):
                acc = tap[0] * win[t + 6]
                for j in range(1, 7):
                    acc = acc + tap[j] * win[t + 6 - j]
                put(ys, i * ROWS + b * 64 + 8 * t, acc)
            return 0

        lax.fori_loop(0, T // 8, body, 0)
    fac = [factor[8 * m : 8 * m + 8, :] for m in range(M)]

    def step(b, state):
        for u in range(8):
            at = b * 64 + u * 8
            mixed = row(ys, ROWS + at) * row(ys, 2 * ROWS + at)
            state = tuple(f * x + mixed for f, x in zip(fac, state))
        return state

    state = lax.fori_loop(0, T // 8, step, (jnp.zeros((8, 128), F32),) * M)
    for m in range(M):
        ends[8 * m : 8 * m + 8, :] = state[m]


def fore_kernel(ys, factor, coef, incoming, filt, gated_t, scr):
    state = tuple(incoming[8 * m : 8 * m + 8, :] for m in range(M))

    def step(b, state):
        for u in range(4):
            at = b * 32 + u * 8
            mixed = row(ys, ROWS + at) * row(ys, 2 * ROWS + at)
            state = tuple(factor[8 * m : 8 * m + 8, :] * state[m] + mixed for m in range(M))
            terms = [coef[8 * m : 8 * m + 8, :] * state[m] for m in range(M)]
            while len(terms) > 1:
                terms = [a + b for a, b in zip(terms[::2], terms[1::2])]
            put(filt, at, terms[0])
            put(scr, at, terms[0] * row(ys, at))
        return state

    lax.fori_loop(0, T // 4, step, state)
    for s in range(8):
        block = scr[pl.ds(s, T, stride=8), :]
        turned = block.T.astype(BF)
        for n in range(8):
            at = 64 * s + 16 * (n // 2)
            gated_t[n % 2, at : at + 16, :] = turned[16 * n : 16 * n + 16, :]


def back_kernel(up, ys, filt, factor, gf, gq, firsts, scr):
    for g in range(T // 16):
        for s in range(8):
            scr[pl.ds(128 * g + s, 16, stride=8), :] = up[16 * g : 16 * g + 16, 128 * s : 128 * s + 128]
    fac = [factor[8 * m : 8 * m + 8, :] for m in range(M)]

    def step(b, state):
        for u in range(8):
            at = ROWS - 8 - b * 64 - u * 8
            upv = row(scr, at)
            grad = upv * row(ys, at)
            put(gf, at, grad)
            put(gq, at, upv * row(filt, at))
            state = tuple(f * x + grad for f, x in zip(fac, state))
        return state

    state = lax.fori_loop(0, T // 8, step, (jnp.zeros((8, 128), F32),) * M)
    for m in range(M):
        firsts[8 * m : 8 * m + 8, :] = state[m]


def tree(terms):
    while len(terms) > 1:
        terms = [a + b for a, b in zip(terms[::2], terms[1::2])]
    return terms[0]


def last_kernel(gf, gq, ys, xs, halo, outgoing, factor, coef, inverse, norm, taps, oq, ok, ov, sums, gs, res):
    adj = [outgoing[8 * m : 8 * m + 8, :] for m in range(M)]
    for n in range(6):
        mix = tree([coef[8 * m : 8 * m + 8, :] * adj[m] for m in range(M)])
        put(gs, ROWS + 8 * n, halo[PAD + 8 * n : PAD + 8 * n + 8, :])
        put(gs, XR + ROWS + 8 * n, mix * halo[3 * PAD + 8 * n : 3 * PAD + 8 * n + 8, :])
        put(gs, 2 * XR + ROWS + 8 * n, mix * halo[2 * PAD + 8 * n : 2 * PAD + 8 * n + 8, :])
        if n < 5:
            first = halo[8 * n : 8 * n + 8, :]
            adj = [(adj[m] - first) * inverse[8 * m : 8 * m + 8, :] for m in range(M)]
    half = M // 2
    for part in range(2):
        ms = range(part * half, (part + 1) * half)
        adj = tuple(outgoing[8 * m : 8 * m + 8, :] for m in ms)
        total = (jnp.zeros((8, 128), F32),) * half

        def step(b, carry):
            adj, total = carry
            for u in range(4):
                at = ROWS - 8 - b * 32 - u * 8
                grad = row(gf, at)
                ks, vs = row(ys, ROWS + at), row(ys, 2 * ROWS + at)
                mixed = ks * vs
                adj = tuple(factor[8 * m : 8 * m + 8, :] * a + grad for m, a in zip(ms, adj))
                total = tuple(t + mixed * a for t, a in zip(total, adj))
                mix = tree([coef[8 * m : 8 * m + 8, :] * a for m, a in zip(ms, adj)])
                if part == 0:
                    put(res, at, mix)
                else:
                    mix = mix + row(res, at)
                    put(gs, at, row(gq, at))
                    put(gs, XR + at, mix * vs)
                    put(gs, 2 * XR + at, mix * ks)
            return adj, total

        adj, total = lax.fori_loop(0, T // 4, step, (adj, total))
        for m, t in zip(ms, total):
            sums[21 * 8 + 8 * m : 21 * 8 + 8 * m + 8, :] = t * norm[8 * m : 8 * m + 8, :]
    for i, out in enumerate((oq, ok, ov)):
        tap = [taps[(i * 7 + j) * 8 : (i * 7 + j) * 8 + 8, :] for j in range(7)]

        def body(b, acc):
            at = i * XR + b * 64
            win = [row(gs, at + 8 * d) for d in range(14)]
            field = [row(xs, at + PAD + 8 * d) for d in range(-6, 8)]
            acc = list(acc)
            for t in range(8):
                value = tap[0] * win[t]
                for j in range(1, 7):
                    value = value + tap[j] * win[t + j]
                put(res, b * 64 + 8 * t, value)
                for j in range(7):
                    acc[j] = acc[j] + win[t] * field[t + 6 - j]
            return tuple(acc)

        acc = lax.fori_loop(0, T // 8, body, (jnp.zeros((8, 128), F32),) * 7)
        for j in range(7):
            sums[(i * 7 + j) * 8 : (i * 7 + j) * 8 + 8, :] = acc[j]
        for g in range(T // 16):
            for s in range(8):
                val = res[pl.ds(128 * g + s, 16, stride=8), :]
                out[16 * g : 16 * g + 16, 128 * s : 128 * s + 128] = val.astype(BF)


def sds(*shape, dtype=F32):
    return jax.ShapeDtypeStruct(shape, dtype)


def shifted(value, steps):
    n = 64
    first, last = max(0, -steps), min(n, n - steps)
    return lax.ppermute(value, CTX, [(i, i + steps) for i in range(first, last)])


def swapped(value, axis):
    return lax.ppermute(value, axis, [(0, 1), (1, 0)])


def carry_weights(rate, forward):
    plan = []
    for axis, n, stride in LEVELS:
        mine = lax.axis_index(axis)
        j = jnp.arange(n)
        if forward:
            inside, lag, all_lag, here = j < mine, mine - 1 - j, n - 1 - j, mine
        else:
            inside, lag, all_lag, here = j > mine, j - 1 - mine, j, n - 1 - mine
        unit = rate * (T * stride)
        lag = jnp.maximum(lag, 0).astype(F32)[:, None, None]
        prefix = jnp.where(inside[:, None, None], jnp.exp(-unit * lag), 0.0)
        whole = jnp.exp(-unit * all_lag.astype(F32)[:, None, None])
        decay = jnp.exp(-unit * here.astype(F32))
        plan.append((axis, prefix, whole, decay))
    return plan


def carried(ends, plan):
    scale, result = None, None
    for level, (axis, prefix, whole, decay) in enumerate(plan):
        parts = lax.all_gather(ends, axis)
        entering = jnp.sum(prefix * parts, axis=0)
        result = entering if level == 0 else result + scale * entering
        scale = decay if level == 0 else scale * decay
        ends = jnp.sum(whole * parts, axis=0)
    return result


def shards(query_proj, key_proj, value_proj, grad_out, out_weight, short_taps, residues, decay_rate):
    q, k, v, go = query_proj[0], key_proj[0], value_proj[0], grad_out[0]
    core = lax.axis_index("core")
    mine_w = lax.all_to_all(jnp.broadcast_to(out_weight, (32, 16, D)), GRP, 0, 0)
    other_w = swapped(mine_w, "core")
    weight = jnp.where(
        core == 0, jnp.stack([mine_w, other_w], axis=1), jnp.stack([other_w, mine_w], axis=1)
    ).reshape(C, D)

    tail = jnp.stack([q[T - 8 :], k[T - 8 :], v[T - 8 :]])
    behind = shifted(tail, 1).astype(F32).reshape(3 * PAD, 128)

    rate = decay_rate.T.reshape(M * 8, 128)
    factor = jnp.exp(-rate)
    norm = jnp.sqrt(-jnp.expm1(-2.0 * rate))
    coef = residues.T.reshape(M * 8, 128) * norm
    taps = jnp.transpose(short_taps, (0, 2, 1)).reshape(21 * 8, 128)

    xs, ys, ends = call(
        shape_kernel, [sds(3 * XR, 128), sds(3 * ROWS, 128), sds(M * 8, 128)], (q, k, v, behind, taps, factor)
    )
    incoming = carried(ends, carry_weights(rate, True))
    filt, gated_t = call(
        fore_kernel,
        [sds(ROWS, 128), sds(2, 512, T, dtype=BF)],
        (ys, factor, coef, incoming),
        [pltpu.VMEM((ROWS, 128), F32)],
    )
    theirs = lax.dynamic_index_in_dim(gated_t, 1 - core, 0, keepdims=False)
    mine = lax.dynamic_index_in_dim(gated_t, core, 0, keepdims=False)
    sent = jnp.dot(theirs, go, preferred_element_type=F32).astype(BF)
    got = swapped(sent, "core")
    kept = (jnp.dot(mine, go, preferred_element_type=F32) + got.astype(F32)).astype(BF)
    pieces = lax.all_to_all(kept.reshape(32, 16, D), GRP, 0, 0)
    summed = jnp.sum(pieces.astype(F32), axis=0).astype(BF)
    weight_grad = summed.astype(F32) + swapped(summed, "yh").astype(F32)

    upstream = lax.dot_general(go, weight, (((1,), (1,)), ((), ())), preferred_element_type=F32)
    gf, gq, firsts = call(
        back_kernel,
        [sds(ROWS, 128), sds(ROWS, 128), sds(M * 8, 128)],
        (upstream, ys, filt, factor),
        [pltpu.VMEM((ROWS, 128), F32)],
    )
    head = jnp.concatenate([gf[:PAD], gq[:PAD], ys[ROWS : ROWS + PAD], ys[2 * ROWS : 2 * ROWS + PAD]], axis=0)
    ahead = shifted(head, -1)
    outgoing = carried(firsts, carry_weights(rate, False))
    oq, ok, ov, sums = call(
        last_kernel,
        [sds(T, C, dtype=BF)] * 3 + [sds((21 + M) * 8, 128)],
        (gf, gq, ys, xs, ahead, outgoing, factor, coef, jnp.exp(rate), norm, taps),
        [pltpu.VMEM((3 * XR, 128), F32), pltpu.VMEM((ROWS, 128), F32)],
    )
    for axis in ("core", "z", "x", ("yl", "yh")):
        sums = jnp.sum(lax.all_gather(sums, axis), axis=0)
    taps_grad = jnp.transpose(sums[: 21 * 8].reshape(3, 7, C), (0, 2, 1))
    residue_grad = sums[21 * 8 :].reshape(M, C).T
    return (oq[None], ok[None], ov[None], weight_grad, taps_grad, residue_grad)


def solution(mesh):
    grid = Mesh(mesh.devices.reshape(2, 4, 4, 2, 2), ("yl", "x", "z", "core", "yh"))
    stream = P("yh", CTX, None)
    return jax.shard_map(
        shards,
        mesh=grid,
        in_specs=(stream, stream, stream, stream, P(CTX, None), P(), P(), P()),
        out_specs=(stream, stream, stream, P(CTX, None), P(), P()),
        check_vma=False,
    )
```

```python
import jax
import jax.numpy as jnp
from jax import lax
from jax.experimental import pallas as pl
from jax.experimental.pallas import tpu as pltpu
from jax.sharding import Mesh, PartitionSpec as P

BF = jnp.bfloat16
F32 = jnp.float32
T = 128
C = 1024
D = 4096
M = 16
PAD = 64
ROWS = 8 * T
XR = PAD + ROWS
CTX = ("yl", "x", "z", "core")
GRP = ("yl", "x", "z")
XZ = ("x", "z")
WA = 2688
HALF = 152
GA = 1792

VMEM = pl.BlockSpec(memory_space=pltpu.VMEM)


def call(body, outs, ins, scratch=(), flops=10_000_000):
    return pl.pallas_call(
        body,
        out_shape=outs,
        in_specs=[VMEM] * len(ins),
        out_specs=[VMEM] * len(outs),
        scratch_shapes=list(scratch),
        compiler_params=pltpu.CompilerParams(vmem_limit_bytes=16 * 1024 * 1024),
        cost_estimate=pl.CostEstimate(flops=flops, bytes_accessed=4_000_000, transcendentals=0),
    )(*ins)


def row(ref, at):
    return ref[pl.ds(pl.multiple_of(at, 8), 8), :]


def put(ref, at, value):
    ref[pl.ds(pl.multiple_of(at, 8), 8), :] = value


def shape_kernel(q, k, v, halo, taps, factor, xs, ys, ends):
    for i, src in enumerate((q, k, v)):
        base = i * XR
        xs[base : base + PAD, :] = halo[i * PAD : (i + 1) * PAD, :]
        for g in range(T // 16):
            for s in range(8):
                val = src[16 * g : 16 * g + 16, 128 * s : 128 * s + 128].astype(F32)
                xs[pl.ds(base + PAD + 128 * g + s, 16, stride=8), :] = val
    for i in range(3):
        tap = [taps[(i * 7 + j) * 8 : (i * 7 + j) * 8 + 8, :] for j in range(7)]

        def body(b, _):
            at = i * XR + PAD + b * 64
            win = [row(xs, at + 8 * d) for d in range(-6, 8)]
            for t in range(8):
                acc = tap[0] * win[t + 6]
                for j in range(1, 7):
                    acc = acc + tap[j] * win[t + 6 - j]
                put(ys, i * ROWS + b * 64 + 8 * t, acc)
            return 0

        lax.fori_loop(0, T // 8, body, 0)
    fac = [factor[8 * m : 8 * m + 8, :] for m in range(M)]

    def step(b, state):
        for u in range(8):
            at = b * 64 + u * 8
            mixed = row(ys, ROWS + at) * row(ys, 2 * ROWS + at)
            state = tuple(f * x + mixed for f, x in zip(fac, state))
        return state

    state = lax.fori_loop(0, T // 8, step, (jnp.zeros((8, 128), F32),) * M)
    for m in range(M):
        ends[8 * m : 8 * m + 8, :] = state[m]


def tree(terms):
    while len(terms) > 1:
        terms = [a + b for a, b in zip(terms[::2], terms[1::2])]
    return terms[0]


def back_kernel(core, up_mine, up_theirs, ys, ends, factor, up, gf, packed, scr):
    zero = core[0] == 0
    for s in range(8):
        half = jnp.where(core[1] == s // 4, 0, 256)
        blocks = []
        for n in range(4):
            at = pl.ds(pl.multiple_of(half + 64 * (s % 4) + 16 * n, 16), 16)
            one, two = up_mine[at, :], up_theirs[at, :]
            blocks += [jnp.where(zero, one, two), jnp.where(zero, two, one)]
        up[pl.ds(s, T, stride=8), :] = jnp.concatenate(blocks, axis=0).T
    fac = [factor[8 * m : 8 * m + 8, :] for m in range(M)]

    def step(b, state):
        for u in range(8):
            at = ROWS - 8 - b * 64 - u * 8
            grad = row(up, at) * row(ys, at)
            put(gf, at, grad)
            state = tuple(f * x + grad for f, x in zip(fac, state))
        return state

    state = lax.fori_loop(0, T // 8, step, (jnp.zeros((8, 128), F32),) * M)
    for m in range(M):
        scr[8 * m : 8 * m + 8, :] = state[m]
    for n in range(2):
        packed[pl.ds(n, 64, stride=4), :] = ends[pl.ds(n, 64, stride=2), :]
        packed[pl.ds(2 + n, 64, stride=4), :] = scr[pl.ds(n, 64, stride=2), :]


def scan_kernel(parts, span, out):
    decay = span[0:2, :]
    state = jnp.zeros((2, 128), F32)
    for b in range(64):
        out[4 * b : 4 * b + 2, :] = state
        state = decay * state + parts[4 * b : 4 * b + 2, :]
    state = jnp.zeros((2, 128), F32)
    for b in range(63, -1, -1):
        out[4 * b + 2 : 4 * b + 4, :] = state
        state = decay * state + parts[4 * b + 2 : 4 * b + 4, :]


def fore_kernel(ys, factor, coef, carries, filt, gated_t, final, scr):
    for n in range(2):
        final[pl.ds(n, 64, stride=2), :] = carries[pl.ds(n, 64, stride=4), :]
    state = tuple(final[8 * m : 8 * m + 8, :] for m in range(M))

    def step(b, state):
        for u in range(4):
            at = b * 32 + u * 8
            mixed = row(ys, ROWS + at) * row(ys, 2 * ROWS + at)
            state = tuple(factor[8 * m : 8 * m + 8, :] * state[m] + mixed for m in range(M))
            value = tree([coef[8 * m : 8 * m + 8, :] * state[m] for m in range(M)])
            put(filt, at, value)
            put(scr, at, value * row(ys, at))
        return state

    state = lax.fori_loop(0, T // 4, step, state)
    for m in range(M):
        final[8 * m : 8 * m + 8, :] = state[m]
    for s in range(8):
        turned = scr[pl.ds(s, T, stride=8), :].T.astype(BF)
        for n in range(8):
            at = 64 * s + 16 * (n // 2)
            gated_t[n % 2, at : at + 16, :] = turned[16 * n : 16 * n + 16, :]


def last_kernel(
    up, gf, filt, ys, xs, halo, final, carries, factor, coef, inverse, norm, taps, oq, ok, ov, sums, gs, res, outgoing
):
    for n in range(2):
        outgoing[pl.ds(n, 64, stride=2), :] = carries[pl.ds(2 + n, 64, stride=4), :]
    sums[37 * 8 :, :] = jnp.zeros((8, 128), F32)
    adj = [outgoing[8 * m : 8 * m + 8, :] for m in range(M)]
    state = [final[8 * m : 8 * m + 8, :] for m in range(M)]
    for n in range(6):
        nup, nq, nk, nv = (halo[i * PAD + 8 * n : i * PAD + 8 * n + 8, :] for i in range(4))
        mixed = nk * nv
        state = [factor[8 * m : 8 * m + 8, :] * state[m] + mixed for m in range(M)]
        value = tree([coef[8 * m : 8 * m + 8, :] * state[m] for m in range(M)])
        mix = tree([coef[8 * m : 8 * m + 8, :] * adj[m] for m in range(M)])
        put(gs, ROWS + 8 * n, nup * value)
        put(gs, XR + ROWS + 8 * n, mix * nv)
        put(gs, 2 * XR + ROWS + 8 * n, mix * nk)
        if n < 5:
            first = nup * nq
            adj = [(adj[m] - first) * inverse[8 * m : 8 * m + 8, :] for m in range(M)]
    for n in range(6, 8):
        for i in range(3):
            put(gs, i * XR + ROWS + 8 * n, jnp.zeros((8, 128), F32))
    half = M // 2
    for part in range(2):
        ms = range(part * half, (part + 1) * half)
        adj = tuple(outgoing[8 * m : 8 * m + 8, :] for m in ms)
        total = (jnp.zeros((8, 128), F32),) * half

        def step(b, carry):
            adj, total = carry
            for u in range(4):
                at = ROWS - 8 - b * 32 - u * 8
                grad = row(gf, at)
                ks, vs = row(ys, ROWS + at), row(ys, 2 * ROWS + at)
                mixed = ks * vs
                adj = tuple(factor[8 * m : 8 * m + 8, :] * a + grad for m, a in zip(ms, adj))
                total = tuple(t + mixed * a for t, a in zip(total, adj))
                mix = tree([coef[8 * m : 8 * m + 8, :] * a for m, a in zip(ms, adj)])
                if part == 0:
                    put(res, at, mix)
                else:
                    mix = mix + row(res, at)
                    put(gs, at, row(up, at) * row(filt, at))
                    put(gs, XR + at, mix * vs)
                    put(gs, 2 * XR + at, mix * ks)
            return adj, total

        adj, total = lax.fori_loop(0, T // 4, step, (adj, total))
        for m, t in zip(ms, total):
            sums[21 * 8 + 8 * m : 21 * 8 + 8 * m + 8, :] = t * norm[8 * m : 8 * m + 8, :]
    for i, out in enumerate((oq, ok, ov)):
        tap = [taps[(i * 7 + j) * 8 : (i * 7 + j) * 8 + 8, :] for j in range(7)]

        def body(b, acc):
            at = i * XR + b * 64
            win = [row(gs, at + 8 * d) for d in range(14)]
            field = [row(xs, at + PAD + 8 * d) for d in range(-6, 8)]
            acc = list(acc)
            for t in range(8):
                value = tap[0] * win[t]
                for j in range(1, 7):
                    value = value + tap[j] * win[t + j]
                put(res, b * 64 + 8 * t, value)
                for j in range(7):
                    acc[j] = acc[j] + win[t] * field[t + 6 - j]
            return tuple(acc)

        acc = lax.fori_loop(0, T // 8, body, (jnp.zeros((8, 128), F32),) * 7)
        for j in range(7):
            sums[(i * 7 + j) * 8 : (i * 7 + j) * 8 + 8, :] = acc[j]
        for g in range(T // 16):
            for s in range(8):
                val = res[pl.ds(128 * g + s, 16, stride=8), :]
                out[16 * g : 16 * g + 16, 128 * s : 128 * s + 128] = val.astype(BF)


def join_kernel(own, one, two, three, part, other_part, out):
    width = own.shape[1]
    for d in range(16):
        at = slice(16 * d, 16 * d + 16)
        value = own[at, :] + one[at, :].astype(F32) + two[at, :].astype(F32) + three[at, :].astype(F32)
        out[at, 0:width] = value.astype(BF)
        here = slice(16 * d, min(16 * d + 16, HALF))
        rows = max(0, here.stop - here.start)
        sums = jnp.zeros((16, 128), F32)
        if rows > 0:
            sums = part[here, :] + other_part[here, :]
        if 0 < rows < 16:
            sums = jnp.concatenate([sums, jnp.zeros((16 - rows, 128), F32)], axis=0)
        high = sums.astype(BF)
        out[at, width : width + 128] = high
        out[at, width + 128 : width + 256] = (sums - high.astype(F32)).astype(BF)


def sds(*shape, dtype=F32):
    return jax.ShapeDtypeStruct(shape, dtype)


def shifted(value, steps):
    n = 64
    first, last = max(0, -steps), min(n, n - steps)
    return lax.ppermute(value, CTX, [(i, i + steps) for i in range(first, last)])


def swapped(value, axis):
    return lax.ppermute(value, axis, [(0, 1), (1, 0)])


def along_y(value, steps):
    pairs = []
    for y in range(4):
        to = (y + steps) % 4
        pairs.append((y % 2 * 2 + y // 2, to % 2 * 2 + to // 2))
    return lax.ppermute(value, ("yl", "yh"), pairs)


def turned_dot(rows, tokens):
    return lax.dot_general(rows, tokens, (((1,), (1,)), ((), ())), preferred_element_type=F32)


def rounded_dot(rows, columns):
    return jnp.dot(rows, columns, preferred_element_type=F32).astype(BF)


def shards(query_proj, key_proj, value_proj, grad_out, out_weight, short_taps, residues, decay_rate):
    q, k, v, go = query_proj[0], key_proj[0], value_proj[0], grad_out[0]
    core, yl, yh = lax.axis_index("core"), lax.axis_index("yl"), lax.axis_index("yh")
    tail = jnp.stack([q[T - 8 :], k[T - 8 :], v[T - 8 :]])
    behind = shifted(tail, 1).astype(F32).reshape(3 * PAD, 128)

    rate = decay_rate.T.reshape(M * 8, 128)
    factor = jnp.exp(-rate)
    norm = jnp.sqrt(-jnp.expm1(-2.0 * rate))
    coef = residues.T.reshape(M * 8, 128) * norm
    taps = jnp.transpose(short_taps, (0, 2, 1)).reshape(21 * 8, 128)
    place = lax.axis_index(CTX)
    span = jnp.exp(-T * lax.dynamic_slice(rate, (2 * place, 0), (2, 128)))

    xs, ys, ends = call(
        shape_kernel, [sds(3 * XR, 128), sds(3 * ROWS, 128), sds(M * 8, 128)], (q, k, v, behind, taps, factor)
    )
    near = lax.all_to_all(jnp.broadcast_to(out_weight[:, :WA], (16, 16, WA)), XZ, 0, 0)
    late = out_weight[:, WA:]
    late = jnp.stack([late, swapped(late, "yl")])
    near, ends = lax.optimization_barrier((near, ends))
    far_low, far_high = along_y(near[:8], 1), along_y(near[8:], -1)
    late = lax.all_to_all(jnp.broadcast_to(late, (16, 2, 16, D - WA)), XZ, 0, 0).reshape(512, D - WA)
    go_theirs = swapped(go, "core")
    go_both = jnp.concatenate([go, go_theirs], axis=0)

    early, rest = go_both[:, :WA], go_both[:, WA:]
    product = [turned_dot(part.reshape(-1, WA), early) for part in (near, far_low, far_high)]
    last = turned_dot(late, rest).reshape(16, 2, 16, 2 * T)
    up_both = jnp.concatenate(product, axis=0) + jnp.swapaxes(last, 0, 1).reshape(512, 2 * T)
    up_mine, up_theirs = up_both[:, :T], swapped(up_both[:, T:], "core")
    up, gf, packed = pl.pallas_call(
        back_kernel,
        out_shape=[sds(ROWS, 128), sds(ROWS, 128), sds(256, 128)],
        in_specs=[pl.BlockSpec(memory_space=pltpu.SMEM)] + [VMEM] * 5,
        out_specs=[VMEM] * 3,
        scratch_shapes=[pltpu.VMEM((M * 8, 128), F32)],
        compiler_params=pltpu.CompilerParams(vmem_limit_bytes=16 * 1024 * 1024),
        cost_estimate=pl.CostEstimate(flops=10_000_000, bytes_accessed=4_000_000, transcendentals=0),
    )(jnp.stack([core, yl]), up_mine, up_theirs, ys, ends, factor)
    head = jnp.concatenate([up[:PAD], ys[:PAD], ys[ROWS : ROWS + PAD], ys[2 * ROWS : 2 * ROWS + PAD]], axis=0)
    ahead = shifted(head, -1)
    blocks = lax.all_to_all(packed.reshape(64, 4, 128), CTX, 0, 0).reshape(256, 128)
    blocks, ahead = lax.optimization_barrier((blocks, ahead))
    (scanned,) = call(scan_kernel, [sds(256, 128)], (blocks, span))
    carries = lax.all_to_all(scanned.reshape(64, 4, 128), CTX, 0, 0).reshape(256, 128)
    filt, gated_t, final = call(
        fore_kernel,
        [sds(ROWS, 128), sds(2, 512, T, dtype=BF), sds(M * 8, 128)],
        (ys, factor, coef, carries),
        [pltpu.VMEM((ROWS, 128), F32)],
    )
    gated_theirs = swapped(lax.dynamic_index_in_dim(gated_t, 1 - core, 0, keepdims=False), "core")
    gated_mine = lax.dynamic_index_in_dim(gated_t, core, 0, keepdims=False)
    gated = jnp.concatenate([gated_mine, gated_theirs], axis=1).reshape(2, 256, 2 * T)
    ours = lax.dynamic_index_in_dim(gated, yl, 0, keepdims=False)
    others = lax.dynamic_index_in_dim(gated, 1 - yl, 0, keepdims=False)
    part_a = GA // 2
    here = lax.dynamic_slice(go_both, (0, part_a * yh), (2 * T, part_a))
    there = lax.dynamic_slice(go_both, (0, part_a * (1 - yh)), (2 * T, part_a))
    parts = [rounded_dot(ours, there), rounded_dot(others, here), rounded_dot(others, there)]
    *parts, gated = lax.optimization_barrier((*parts, gated))
    got = [
        lax.ppermute(parts[0], ("yl", "yh"), [(0, 1), (1, 0), (2, 3), (3, 2)]),
        lax.ppermute(parts[1], ("yl", "yh"), [(0, 2), (2, 0), (1, 3), (3, 1)]),
        lax.ppermute(parts[2], ("yl", "yh"), [(0, 3), (3, 0), (1, 2), (2, 1)]),
    ]
    spread = rounded_dot(jnp.swapaxes(gated.reshape(2, 16, 16, 2 * T), 0, 1).reshape(512, 2 * T), go_both[:, GA:])
    spread = lax.all_to_all(spread.reshape(16, 2, 16, D - GA), XZ, 0, 0)
    first = jnp.dot(ours, here, preferred_element_type=F32)
    up, *got = lax.optimization_barrier((up, *got))
    oq, ok, ov, sums = call(
        last_kernel,
        [sds(T, C, dtype=BF)] * 3 + [sds(304, 128)],
        (up, gf, filt, ys, xs, ahead, final, carries, factor, coef, jnp.exp(rate), norm, taps),
        [pltpu.VMEM((3 * XR, 128), F32), pltpu.VMEM((ROWS, 128), F32), pltpu.VMEM((M * 8, 128), F32)],
    )
    halves = sums.reshape(2, HALF, 128)
    part = lax.dynamic_index_in_dim(halves, core, 0, keepdims=False)
    other_part = swapped(lax.dynamic_index_in_dim(halves, 1 - core, 0, keepdims=False), "core")
    (joined,) = call(join_kernel, [sds(256, part_a + 256, dtype=BF)], (first, *got, part, other_part))
    joined, spread = lax.optimization_barrier((joined, spread))
    joined = lax.all_to_all(joined.reshape(16, 16, part_a + 256), XZ, 0, 0)
    spread = jnp.sum(spread.astype(F32), axis=0).astype(BF)
    near = lax.dynamic_index_in_dim(spread, yl, 0, keepdims=False)
    far = lax.dynamic_index_in_dim(spread, 1 - yl, 0, keepdims=False)
    levels = [
        swapped(near, "yh"),
        lax.ppermute(far, ("yl", "yh"), [(0, 2), (2, 0), (1, 3), (3, 1)]),
        lax.ppermute(far, ("yl", "yh"), [(0, 3), (3, 0), (1, 2), (2, 1)]),
    ]
    joined, *levels = lax.optimization_barrier((joined, *levels))
    joined = jnp.sum(joined.astype(F32), axis=0)
    first = joined[:, :part_a]
    first_other = swapped(first, "yh")
    part = joined[:, part_a : part_a + 128] + joined[:, part_a + 128 :]
    part = lax.all_to_all(jnp.broadcast_to(part, (64, 16, 128)), ("yl", "yh", "x", "z"), 0, 0)
    part = jnp.sum(part.reshape(4, 256, 128)[:, :HALF], axis=0)
    rest = swapped(part, "core")
    level = (near.astype(F32) + levels[0].astype(F32)) + (levels[1].astype(F32) + levels[2].astype(F32))
    weight_grad = jnp.concatenate(
        [jnp.where(yh == 0, first, first_other), jnp.where(yh == 0, first_other, first), level], axis=1
    )
    sums = jnp.where(core == 0, jnp.concatenate([part, rest], axis=0), jnp.concatenate([rest, part], axis=0))
    taps_grad = jnp.transpose(sums[: 21 * 8].reshape(3, 7, C), (0, 2, 1))
    residue_grad = sums[21 * 8 : 37 * 8].reshape(M, C).T
    return (oq[None], ok[None], ov[None], weight_grad, taps_grad, residue_grad)


def solution(mesh):
    grid = Mesh(mesh.devices.reshape(2, 4, 4, 2, 2), ("yl", "x", "z", "core", "yh"))
    stream = P("yh", CTX, None)
    return jax.shard_map(
        shards,
        mesh=grid,
        in_specs=(stream, stream, stream, stream, P(CTX, None), P(), P(), P()),
        out_specs=(stream, stream, stream, P(CTX, None), P(), P()),
        check_vma=False,
    )
```

```python
import jax
import jax.numpy as jnp
from jax import lax
from jax.experimental import pallas as pl
from jax.experimental.pallas import tpu as pltpu
from jax.sharding import Mesh, PartitionSpec as P

BF = jnp.bfloat16
F32 = jnp.float32
T = 128
C = 1024
D = 4096
M = 16
PAD = 64
ROWS = 8 * T
XR = PAD + ROWS
CTX = ("yl", "x", "z", "core")
GRP = ("yl", "x", "z")
XZ = ("x", "z")
WA = 2688
LAST = 7_000_000_000
HALF = 152
GA = 1792

VMEM = pl.BlockSpec(memory_space=pltpu.VMEM)


def call(body, outs, ins, scratch=(), flops=10_000_000):
    return pl.pallas_call(
        body,
        out_shape=outs,
        in_specs=[VMEM] * len(ins),
        out_specs=[VMEM] * len(outs),
        scratch_shapes=list(scratch),
        compiler_params=pltpu.CompilerParams(vmem_limit_bytes=16 * 1024 * 1024),
        cost_estimate=pl.CostEstimate(flops=flops, bytes_accessed=4_000_000, transcendentals=0),
    )(*ins)


def row(ref, at):
    return ref[pl.ds(pl.multiple_of(at, 8), 8), :]


def put(ref, at, value):
    ref[pl.ds(pl.multiple_of(at, 8), 8), :] = value


def shape_kernel(q, k, v, halo, taps, factor, xs, ys, ends):
    for i, src in enumerate((q, k, v)):
        base = i * XR
        xs[base : base + PAD, :] = halo[i * PAD : (i + 1) * PAD, :]
        for g in range(T // 16):
            for s in range(8):
                val = src[16 * g : 16 * g + 16, 128 * s : 128 * s + 128].astype(F32)
                xs[pl.ds(base + PAD + 128 * g + s, 16, stride=8), :] = val
    for i in range(3):
        tap = [taps[(i * 7 + j) * 8 : (i * 7 + j) * 8 + 8, :] for j in range(7)]

        def body(b, _):
            at = i * XR + PAD + b * 64
            win = [row(xs, at + 8 * d) for d in range(-6, 8)]
            for t in range(8):
                acc = tap[0] * win[t + 6]
                for j in range(1, 7):
                    acc = acc + tap[j] * win[t + 6 - j]
                put(ys, i * ROWS + b * 64 + 8 * t, acc)
            return 0

        lax.fori_loop(0, T // 8, body, 0)
    fac = [factor[8 * m : 8 * m + 8, :] for m in range(M)]

    def step(b, state):
        for u in range(8):
            at = b * 64 + u * 8
            mixed = row(ys, ROWS + at) * row(ys, 2 * ROWS + at)
            state = tuple(f * x + mixed for f, x in zip(fac, state))
        return state

    state = lax.fori_loop(0, T // 8, step, (jnp.zeros((8, 128), F32),) * M)
    for m in range(M):
        ends[8 * m : 8 * m + 8, :] = state[m]


def tree(terms):
    while len(terms) > 1:
        terms = [a + b for a, b in zip(terms[::2], terms[1::2])]
    return terms[0]


def back_kernel(core, up_mine, up_theirs, ys, ends, factor, up, packed, scr):
    zero = core[0] == 0
    for s in range(8):
        half = jnp.where(core[1] == s // 4, 0, 256)
        blocks = []
        for n in range(4):
            at = pl.ds(pl.multiple_of(half + 64 * (s % 4) + 16 * n, 16), 16)
            one, two = up_mine[at, :], up_theirs[at, :]
            blocks += [jnp.where(zero, one, two), jnp.where(zero, two, one)]
        up[pl.ds(s, T, stride=8), :] = jnp.concatenate(blocks, axis=0).T
    fac = [factor[8 * m : 8 * m + 8, :] for m in range(M)]

    def step(b, state):
        for u in range(8):
            at = ROWS - 8 - b * 64 - u * 8
            grad = row(up, at) * row(ys, at)
            state = tuple(f * x + grad for f, x in zip(fac, state))
        return state

    state = lax.fori_loop(0, T // 8, step, (jnp.zeros((8, 128), F32),) * M)
    for m in range(M):
        scr[8 * m : 8 * m + 8, :] = state[m]
    for n in range(2):
        packed[pl.ds(n, 64, stride=4), :] = ends[pl.ds(n, 64, stride=2), :]
        packed[pl.ds(2 + n, 64, stride=4), :] = scr[pl.ds(n, 64, stride=2), :]


def scan_kernel(parts, span, out):
    decay = span[0:2, :]
    state = jnp.zeros((2, 128), F32)
    for b in range(64):
        out[4 * b : 4 * b + 2, :] = state
        state = decay * state + parts[4 * b : 4 * b + 2, :]
    state = jnp.zeros((2, 128), F32)
    for b in range(63, -1, -1):
        out[4 * b + 2 : 4 * b + 4, :] = state
        state = decay * state + parts[4 * b + 2 : 4 * b + 4, :]


def fore_kernel(ys, factor, coef, carries, filt, gated_t, final, scr):
    for n in range(2):
        final[pl.ds(n, 64, stride=2), :] = carries[pl.ds(n, 64, stride=4), :]
    state = tuple(final[8 * m : 8 * m + 8, :] for m in range(M))

    def step(b, state):
        for u in range(4):
            at = b * 32 + u * 8
            mixed = row(ys, ROWS + at) * row(ys, 2 * ROWS + at)
            state = tuple(factor[8 * m : 8 * m + 8, :] * state[m] + mixed for m in range(M))
            value = tree([coef[8 * m : 8 * m + 8, :] * state[m] for m in range(M)])
            put(filt, at, value)
            put(scr, at, value * row(ys, at))
        return state

    state = lax.fori_loop(0, T // 4, step, state)
    for m in range(M):
        final[8 * m : 8 * m + 8, :] = state[m]
    for s in range(8):
        turned = scr[pl.ds(s, T, stride=8), :].T.astype(BF)
        for n in range(8):
            at = 64 * s + 16 * (n // 2)
            gated_t[n % 2, at : at + 16, :] = turned[16 * n : 16 * n + 16, :]


def last_kernel(
    up, filt, ys, xs, halo, final, carries, factor, coef, inverse, norm, taps, oq, ok, ov, sums, gs, res, outgoing
):
    for n in range(2):
        outgoing[pl.ds(n, 64, stride=2), :] = carries[pl.ds(2 + n, 64, stride=4), :]
    sums[37 * 8 :, :] = jnp.zeros((8, 128), F32)
    adj = [outgoing[8 * m : 8 * m + 8, :] for m in range(M)]
    state = [final[8 * m : 8 * m + 8, :] for m in range(M)]
    for n in range(6):
        nup, nq, nk, nv = (halo[i * PAD + 8 * n : i * PAD + 8 * n + 8, :] for i in range(4))
        mixed = nk * nv
        state = [factor[8 * m : 8 * m + 8, :] * state[m] + mixed for m in range(M)]
        value = tree([coef[8 * m : 8 * m + 8, :] * state[m] for m in range(M)])
        mix = tree([coef[8 * m : 8 * m + 8, :] * adj[m] for m in range(M)])
        put(gs, ROWS + 8 * n, nup * value)
        put(gs, XR + ROWS + 8 * n, mix * nv)
        put(gs, 2 * XR + ROWS + 8 * n, mix * nk)
        if n < 5:
            first = nup * nq
            adj = [(adj[m] - first) * inverse[8 * m : 8 * m + 8, :] for m in range(M)]
    for n in range(6, 8):
        for i in range(3):
            put(gs, i * XR + ROWS + 8 * n, jnp.zeros((8, 128), F32))
    half = M // 2
    for part in range(2):
        ms = range(part * half, (part + 1) * half)
        adj = tuple(outgoing[8 * m : 8 * m + 8, :] for m in ms)
        total = (jnp.zeros((8, 128), F32),) * half

        def step(b, carry):
            adj, total = carry
            for u in range(4):
                at = ROWS - 8 - b * 32 - u * 8
                grad = row(up, at) * row(ys, at)
                ks, vs = row(ys, ROWS + at), row(ys, 2 * ROWS + at)
                mixed = ks * vs
                adj = tuple(factor[8 * m : 8 * m + 8, :] * a + grad for m, a in zip(ms, adj))
                total = tuple(t + mixed * a for t, a in zip(total, adj))
                mix = tree([coef[8 * m : 8 * m + 8, :] * a for m, a in zip(ms, adj)])
                if part == 0:
                    put(res, at, mix)
                else:
                    mix = mix + row(res, at)
                    put(gs, at, row(up, at) * row(filt, at))
                    put(gs, XR + at, mix * vs)
                    put(gs, 2 * XR + at, mix * ks)
            return adj, total

        adj, total = lax.fori_loop(0, T // 4, step, (adj, total))
        for m, t in zip(ms, total):
            sums[21 * 8 + 8 * m : 21 * 8 + 8 * m + 8, :] = t * norm[8 * m : 8 * m + 8, :]
    for i, out in enumerate((oq, ok, ov)):
        tap = [taps[(i * 7 + j) * 8 : (i * 7 + j) * 8 + 8, :] for j in range(7)]

        def body(b, acc):
            at = i * XR + b * 64
            win = [row(gs, at + 8 * d) for d in range(14)]
            field = [row(xs, at + PAD + 8 * d) for d in range(-6, 8)]
            acc = list(acc)
            for t in range(8):
                value = tap[0] * win[t]
                for j in range(1, 7):
                    value = value + tap[j] * win[t + j]
                put(res, b * 64 + 8 * t, value)
                for j in range(7):
                    acc[j] = acc[j] + win[t] * field[t + 6 - j]
            return tuple(acc)

        acc = lax.fori_loop(0, T // 8, body, (jnp.zeros((8, 128), F32),) * 7)
        for j in range(7):
            sums[(i * 7 + j) * 8 : (i * 7 + j) * 8 + 8, :] = acc[j]
        for g in range(T // 16):
            for s in range(8):
                val = res[pl.ds(128 * g + s, 16, stride=8), :]
                out[16 * g : 16 * g + 16, 128 * s : 128 * s + 128] = val.astype(BF)


def join_kernel(own, one, two, three, part, other_part, out):
    width = own.shape[1]
    for d in range(16):
        at = slice(16 * d, 16 * d + 16)
        value = own[at, :] + one[at, :].astype(F32) + two[at, :].astype(F32) + three[at, :].astype(F32)
        out[at, 0:width] = value.astype(BF)
        here = slice(16 * d, min(16 * d + 16, HALF))
        rows = max(0, here.stop - here.start)
        sums = jnp.zeros((16, 128), F32)
        if rows > 0:
            sums = part[here, :] + other_part[here, :]
        if 0 < rows < 16:
            sums = jnp.concatenate([sums, jnp.zeros((16 - rows, 128), F32)], axis=0)
        high = sums.astype(BF)
        out[at, width : width + 128] = high
        out[at, width + 128 : width + 256] = (sums - high.astype(F32)).astype(BF)


def sds(*shape, dtype=F32):
    return jax.ShapeDtypeStruct(shape, dtype)


def shifted(value, steps):
    n = 64
    first, last = max(0, -steps), min(n, n - steps)
    return lax.ppermute(value, CTX, [(i, i + steps) for i in range(first, last)])


def swapped(value, axis):
    return lax.ppermute(value, axis, [(0, 1), (1, 0)])


def along_y(value, steps):
    pairs = []
    for y in range(4):
        to = (y + steps) % 4
        pairs.append((y % 2 * 2 + y // 2, to % 2 * 2 + to // 2))
    return lax.ppermute(value, ("yl", "yh"), pairs)


def turned_dot(rows, tokens):
    return lax.dot_general(rows, tokens, (((1,), (1,)), ((), ())), preferred_element_type=F32)


def rounded_dot(rows, columns):
    return jnp.dot(rows, columns, preferred_element_type=F32).astype(BF)


def shards(query_proj, key_proj, value_proj, grad_out, out_weight, short_taps, residues, decay_rate):
    q, k, v, go = query_proj[0], key_proj[0], value_proj[0], grad_out[0]
    core, yl, yh = lax.axis_index("core"), lax.axis_index("yl"), lax.axis_index("yh")
    tail = jnp.stack([q[T - 8 :], k[T - 8 :], v[T - 8 :]])
    behind = shifted(tail, 1).astype(F32).reshape(3 * PAD, 128)

    rate = decay_rate.T.reshape(M * 8, 128)
    factor = jnp.exp(-rate)
    norm = jnp.sqrt(-jnp.expm1(-2.0 * rate))
    coef = residues.T.reshape(M * 8, 128) * norm
    taps = jnp.transpose(short_taps, (0, 2, 1)).reshape(21 * 8, 128)
    place = lax.axis_index(CTX)
    span = jnp.exp(-T * lax.dynamic_slice(rate, (2 * place, 0), (2, 128)))

    xs, ys, ends = call(
        shape_kernel, [sds(3 * XR, 128), sds(3 * ROWS, 128), sds(M * 8, 128)], (q, k, v, behind, taps, factor)
    )
    near = lax.all_to_all(jnp.broadcast_to(out_weight[:, :WA], (16, 16, WA)), XZ, 0, 0)
    late = out_weight[:, WA:]
    late = jnp.stack([late, swapped(late, "yl")])
    near, ends = lax.optimization_barrier((near, ends))
    far_low, far_high = along_y(near[:8], 1), along_y(near[8:], -1)
    late = lax.all_to_all(jnp.broadcast_to(late, (16, 2, 16, D - WA)), XZ, 0, 0).reshape(512, D - WA)
    go_theirs = swapped(go, "core")
    go_both = jnp.concatenate([go, go_theirs], axis=0)

    early, rest = go_both[:, :WA], go_both[:, WA:]
    product = [turned_dot(part.reshape(-1, WA), early) for part in (near, far_low, far_high)]
    last = turned_dot(late, rest).reshape(16, 2, 16, 2 * T)
    up_both = jnp.concatenate(product, axis=0) + jnp.swapaxes(last, 0, 1).reshape(512, 2 * T)
    up_mine, up_theirs = up_both[:, :T], swapped(up_both[:, T:], "core")
    up, packed = pl.pallas_call(
        back_kernel,
        out_shape=[sds(ROWS, 128), sds(256, 128)],
        in_specs=[pl.BlockSpec(memory_space=pltpu.SMEM)] + [VMEM] * 5,
        out_specs=[VMEM] * 2,
        scratch_shapes=[pltpu.VMEM((M * 8, 128), F32)],
        compiler_params=pltpu.CompilerParams(vmem_limit_bytes=16 * 1024 * 1024),
        cost_estimate=pl.CostEstimate(flops=10_000_000, bytes_accessed=4_000_000, transcendentals=0),
    )(jnp.stack([core, yl]), up_mine, up_theirs, ys, ends, factor)
    head = jnp.concatenate([up[:PAD], ys[:PAD], ys[ROWS : ROWS + PAD], ys[2 * ROWS : 2 * ROWS + PAD]], axis=0)
    ahead = shifted(head, -1)
    blocks = lax.all_to_all(packed.reshape(64, 4, 128), CTX, 0, 0).reshape(256, 128)
    blocks, ahead = lax.optimization_barrier((blocks, ahead))
    (scanned,) = call(scan_kernel, [sds(256, 128)], (blocks, span))
    carries = lax.all_to_all(scanned.reshape(64, 4, 128), CTX, 0, 0).reshape(256, 128)
    filt, gated_t, final = call(
        fore_kernel,
        [sds(ROWS, 128), sds(2, 512, T, dtype=BF), sds(M * 8, 128)],
        (ys, factor, coef, carries),
        [pltpu.VMEM((ROWS, 128), F32)],
    )
    gated_theirs = swapped(lax.dynamic_index_in_dim(gated_t, 1 - core, 0, keepdims=False), "core")
    gated_mine = lax.dynamic_index_in_dim(gated_t, core, 0, keepdims=False)
    gated = jnp.concatenate([gated_mine, gated_theirs], axis=1).reshape(2, 256, 2 * T)
    ours = lax.dynamic_index_in_dim(gated, yl, 0, keepdims=False)
    others = lax.dynamic_index_in_dim(gated, 1 - yl, 0, keepdims=False)
    part_a = GA // 2
    here = lax.dynamic_slice(go_both, (0, part_a * yh), (2 * T, part_a))
    there = lax.dynamic_slice(go_both, (0, part_a * (1 - yh)), (2 * T, part_a))
    parts = [rounded_dot(ours, there), rounded_dot(others, here), rounded_dot(others, there)]
    got = [
        lax.ppermute(parts[0], ("yl", "yh"), [(0, 1), (1, 0), (2, 3), (3, 2)]),
        lax.ppermute(parts[1], ("yl", "yh"), [(0, 2), (2, 0), (1, 3), (3, 1)]),
        lax.ppermute(parts[2], ("yl", "yh"), [(0, 3), (3, 0), (1, 2), (2, 1)]),
    ]
    spread = rounded_dot(jnp.swapaxes(gated.reshape(2, 16, 16, 2 * T), 0, 1).reshape(512, 2 * T), go_both[:, GA:])
    spread = lax.all_to_all(spread.reshape(16, 2, 16, D - GA), XZ, 0, 0)
    first = jnp.dot(ours, here, preferred_element_type=F32)
    oq, ok, ov, sums = call(
        last_kernel,
        [sds(T, C, dtype=BF)] * 3 + [sds(304, 128)],
        (up, filt, ys, xs, ahead, final, carries, factor, coef, jnp.exp(rate), norm, taps),
        [pltpu.VMEM((3 * XR, 128), F32), pltpu.VMEM((ROWS, 128), F32), pltpu.VMEM((M * 8, 128), F32)],
        flops=LAST,
    )
    halves = sums.reshape(2, HALF, 128)
    part = lax.dynamic_index_in_dim(halves, core, 0, keepdims=False)
    other_part = swapped(lax.dynamic_index_in_dim(halves, 1 - core, 0, keepdims=False), "core")
    (joined,) = call(join_kernel, [sds(256, part_a + 256, dtype=BF)], (first, *got, part, other_part))
    joined, spread = lax.optimization_barrier((joined, spread))
    joined = lax.all_to_all(joined.reshape(16, 16, part_a + 256), XZ, 0, 0)
    spread = jnp.sum(spread.astype(F32), axis=0).astype(BF)
    near = lax.dynamic_index_in_dim(spread, yl, 0, keepdims=False)
    far = lax.dynamic_index_in_dim(spread, 1 - yl, 0, keepdims=False)
    levels = [
        swapped(near, "yh"),
        lax.ppermute(far, ("yl", "yh"), [(0, 2), (2, 0), (1, 3), (3, 1)]),
        lax.ppermute(far, ("yl", "yh"), [(0, 3), (3, 0), (1, 2), (2, 1)]),
    ]
    joined, *levels = lax.optimization_barrier((joined, *levels))
    joined = jnp.sum(joined.astype(F32), axis=0)
    first = joined[:, :part_a]
    first_other = swapped(first, "yh")
    part = joined[:, part_a : part_a + 128] + joined[:, part_a + 128 :]
    part = lax.all_to_all(jnp.broadcast_to(part, (64, 16, 128)), ("yl", "yh", "x", "z"), 0, 0)
    part = jnp.sum(part.reshape(4, 256, 128)[:, :HALF], axis=0)
    rest = swapped(part, "core")
    level = (near.astype(F32) + levels[0].astype(F32)) + (levels[1].astype(F32) + levels[2].astype(F32))
    weight_grad = jnp.concatenate(
        [jnp.where(yh == 0, first, first_other), jnp.where(yh == 0, first_other, first), level], axis=1
    )
    sums = jnp.where(core == 0, jnp.concatenate([part, rest], axis=0), jnp.concatenate([rest, part], axis=0))
    taps_grad = jnp.transpose(sums[: 21 * 8].reshape(3, 7, C), (0, 2, 1))
    residue_grad = sums[21 * 8 : 37 * 8].reshape(M, C).T
    return (oq[None], ok[None], ov[None], weight_grad, taps_grad, residue_grad)


def solution(mesh):
    grid = Mesh(mesh.devices.reshape(2, 4, 4, 2, 2), ("yl", "x", "z", "core", "yh"))
    stream = P("yh", CTX, None)
    return jax.shard_map(
        shards,
        mesh=grid,
        in_specs=(stream, stream, stream, stream, P(CTX, None), P(), P(), P()),
        out_specs=(stream, stream, stream, P(CTX, None), P(), P()),
        check_vma=False,
    )
```

```python
import jax
import jax.numpy as jnp
from jax import lax
from jax.experimental import pallas as pl
from jax.experimental.pallas import tpu as pltpu
from jax.sharding import Mesh, PartitionSpec as P

BF = jnp.bfloat16
F32 = jnp.float32
T = 128
C = 1024
D = 4096
M = 16
PAD = 64
ROWS = 8 * T
XR = PAD + ROWS
CTX = ("yl", "x", "z", "core")
GRP = ("yl", "x", "z")
XZ = ("x", "z")
WA = 2688
LAST = 7_000_000_000
HALF = 152
SHARE = 10
GA = 2048

VMEM = pl.BlockSpec(memory_space=pltpu.VMEM)


def call(body, outs, ins, scratch=(), flops=10_000_000):
    return pl.pallas_call(
        body,
        out_shape=outs,
        in_specs=[VMEM] * len(ins),
        out_specs=[VMEM] * len(outs),
        scratch_shapes=list(scratch),
        compiler_params=pltpu.CompilerParams(vmem_limit_bytes=16 * 1024 * 1024),
        cost_estimate=pl.CostEstimate(flops=flops, bytes_accessed=4_000_000, transcendentals=0),
    )(*ins)


def row(ref, at):
    return ref[pl.ds(pl.multiple_of(at, 8), 8), :]


def put(ref, at, value):
    ref[pl.ds(pl.multiple_of(at, 8), 8), :] = value


def shape_kernel(q, k, v, halo, taps, factor, xs, ys, ends):
    for i, src in enumerate((q, k, v)):
        base = i * XR
        xs[base : base + PAD, :] = halo[i * PAD : (i + 1) * PAD, :]
        for g in range(T // 16):
            for s in range(8):
                val = src[16 * g : 16 * g + 16, 128 * s : 128 * s + 128].astype(F32)
                xs[pl.ds(base + PAD + 128 * g + s, 16, stride=8), :] = val
    for i in range(3):
        tap = [taps[(i * 7 + j) * 8 : (i * 7 + j) * 8 + 8, :] for j in range(7)]

        def body(b, _):
            at = i * XR + PAD + b * 64
            win = [row(xs, at + 8 * d) for d in range(-6, 8)]
            for t in range(8):
                acc = tap[0] * win[t + 6]
                for j in range(1, 7):
                    acc = acc + tap[j] * win[t + 6 - j]
                put(ys, i * ROWS + b * 64 + 8 * t, acc)
            return 0

        lax.fori_loop(0, T // 8, body, 0)
    fac = [factor[8 * m : 8 * m + 8, :] for m in range(M)]

    def step(b, state):
        for u in range(8):
            at = b * 64 + u * 8
            mixed = row(ys, ROWS + at) * row(ys, 2 * ROWS + at)
            state = tuple(f * x + mixed for f, x in zip(fac, state))
        return state

    state = lax.fori_loop(0, T // 8, step, (jnp.zeros((8, 128), F32),) * M)
    for m in range(M):
        ends[8 * m : 8 * m + 8, :] = state[m]


def tree(terms):
    while len(terms) > 1:
        terms = [a + b for a, b in zip(terms[::2], terms[1::2])]
    return terms[0]


def back_kernel(core, up_mine, up_theirs, ys, ends, factor, up, packed, scr):
    zero = core[0] == 0
    for s in range(8):
        half = jnp.where(core[1] == s // 4, 0, 256)
        blocks = []
        for n in range(4):
            at = pl.ds(pl.multiple_of(half + 64 * (s % 4) + 16 * n, 16), 16)
            one, two = up_mine[at, :], up_theirs[at, :]
            blocks += [jnp.where(zero, one, two), jnp.where(zero, two, one)]
        up[pl.ds(s, T, stride=8), :] = jnp.concatenate(blocks, axis=0).T
    fac = [factor[8 * m : 8 * m + 8, :] for m in range(M)]

    def step(b, state):
        for u in range(8):
            at = ROWS - 8 - b * 64 - u * 8
            grad = row(up, at) * row(ys, at)
            state = tuple(f * x + grad for f, x in zip(fac, state))
        return state

    state = lax.fori_loop(0, T // 8, step, (jnp.zeros((8, 128), F32),) * M)
    for m in range(M):
        scr[8 * m : 8 * m + 8, :] = state[m]
    for n in range(2):
        packed[pl.ds(n, 64, stride=4), :] = ends[pl.ds(n, 64, stride=2), :]
        packed[pl.ds(2 + n, 64, stride=4), :] = scr[pl.ds(n, 64, stride=2), :]


def scan_kernel(parts, span, out):
    decay = span[0:2, :]
    state = jnp.zeros((2, 128), F32)
    for b in range(64):
        out[4 * b : 4 * b + 2, :] = state
        state = decay * state + parts[4 * b : 4 * b + 2, :]
    state = jnp.zeros((2, 128), F32)
    for b in range(63, -1, -1):
        out[4 * b + 2 : 4 * b + 4, :] = state
        state = decay * state + parts[4 * b + 2 : 4 * b + 4, :]


def fore_kernel(ys, factor, coef, carries, filt, gated_t, final, scr):
    for n in range(2):
        final[pl.ds(n, 64, stride=2), :] = carries[pl.ds(n, 64, stride=4), :]
    state = tuple(final[8 * m : 8 * m + 8, :] for m in range(M))

    def step(b, state):
        for u in range(4):
            at = b * 32 + u * 8
            mixed = row(ys, ROWS + at) * row(ys, 2 * ROWS + at)
            state = tuple(factor[8 * m : 8 * m + 8, :] * state[m] + mixed for m in range(M))
            value = tree([coef[8 * m : 8 * m + 8, :] * state[m] for m in range(M)])
            put(filt, at, value)
            put(scr, at, value * row(ys, at))
        return state

    state = lax.fori_loop(0, T // 4, step, state)
    for m in range(M):
        final[8 * m : 8 * m + 8, :] = state[m]
    for s in range(8):
        turned = scr[pl.ds(s, T, stride=8), :].T.astype(BF)
        for n in range(8):
            at = 64 * s + 16 * (n // 2)
            gated_t[n % 2, at : at + 16, :] = turned[16 * n : 16 * n + 16, :]


def last_kernel(
    up, filt, ys, xs, halo, final, carries, factor, coef, inverse, norm, taps, oq, ok, ov, sums, gs, res, outgoing
):
    for n in range(2):
        outgoing[pl.ds(n, 64, stride=2), :] = carries[pl.ds(2 + n, 64, stride=4), :]
    sums[37 * 8 :, :] = jnp.zeros((8, 128), F32)
    adj = [outgoing[8 * m : 8 * m + 8, :] for m in range(M)]
    state = [final[8 * m : 8 * m + 8, :] for m in range(M)]
    for n in range(6):
        nup, nq, nk, nv = (halo[i * PAD + 8 * n : i * PAD + 8 * n + 8, :] for i in range(4))
        mixed = nk * nv
        state = [factor[8 * m : 8 * m + 8, :] * state[m] + mixed for m in range(M)]
        value = tree([coef[8 * m : 8 * m + 8, :] * state[m] for m in range(M)])
        mix = tree([coef[8 * m : 8 * m + 8, :] * adj[m] for m in range(M)])
        put(gs, ROWS + 8 * n, nup * value)
        put(gs, XR + ROWS + 8 * n, mix * nv)
        put(gs, 2 * XR + ROWS + 8 * n, mix * nk)
        if n < 5:
            first = nup * nq
            adj = [(adj[m] - first) * inverse[8 * m : 8 * m + 8, :] for m in range(M)]
    for n in range(6, 8):
        for i in range(3):
            put(gs, i * XR + ROWS + 8 * n, jnp.zeros((8, 128), F32))
    half = M // 2
    for part in range(2):
        ms = range(part * half, (part + 1) * half)
        adj = tuple(outgoing[8 * m : 8 * m + 8, :] for m in ms)
        total = (jnp.zeros((8, 128), F32),) * half

        def step(b, carry):
            adj, total = carry
            for u in range(4):
                at = ROWS - 8 - b * 32 - u * 8
                grad = row(up, at) * row(ys, at)
                ks, vs = row(ys, ROWS + at), row(ys, 2 * ROWS + at)
                mixed = ks * vs
                adj = tuple(factor[8 * m : 8 * m + 8, :] * a + grad for m, a in zip(ms, adj))
                total = tuple(t + mixed * a for t, a in zip(total, adj))
                mix = tree([coef[8 * m : 8 * m + 8, :] * a for m, a in zip(ms, adj)])
                if part == 0:
                    put(res, at, mix)
                else:
                    mix = mix + row(res, at)
                    put(gs, at, row(up, at) * row(filt, at))
                    put(gs, XR + at, mix * vs)
                    put(gs, 2 * XR + at, mix * ks)
            return adj, total

        adj, total = lax.fori_loop(0, T // 4, step, (adj, total))
        for m, t in zip(ms, total):
            sums[21 * 8 + 8 * m : 21 * 8 + 8 * m + 8, :] = t * norm[8 * m : 8 * m + 8, :]
    for i, out in enumerate((oq, ok, ov)):
        tap = [taps[(i * 7 + j) * 8 : (i * 7 + j) * 8 + 8, :] for j in range(7)]

        def body(b, acc):
            at = i * XR + b * 64
            win = [row(gs, at + 8 * d) for d in range(14)]
            field = [row(xs, at + PAD + 8 * d) for d in range(-6, 8)]
            acc = list(acc)
            for t in range(8):
                value = tap[0] * win[t]
                for j in range(1, 7):
                    value = value + tap[j] * win[t + j]
                put(res, b * 64 + 8 * t, value)
                for j in range(7):
                    acc[j] = acc[j] + win[t] * field[t + 6 - j]
            return tuple(acc)

        acc = lax.fori_loop(0, T // 8, body, (jnp.zeros((8, 128), F32),) * 7)
        for j in range(7):
            sums[(i * 7 + j) * 8 : (i * 7 + j) * 8 + 8, :] = acc[j]
        for g in range(T // 16):
            for s in range(8):
                val = res[pl.ds(128 * g + s, 16, stride=8), :]
                out[16 * g : 16 * g + 16, 128 * s : 128 * s + 128] = val.astype(BF)


def join_kernel(own, one, two, three, part, other_part, out):
    width = own.shape[1]
    for d in range(16):
        at = slice(16 * d, 16 * d + 16)
        value = own[at, :] + one[at, :].astype(F32) + two[at, :].astype(F32) + three[at, :].astype(F32)
        out[at, 0:width] = value.astype(BF)
        here = slice(SHARE * d, min(SHARE * d + SHARE, HALF))
        rows = max(0, here.stop - here.start)
        sums = jnp.zeros((16, 128), F32)
        if rows > 0:
            sums = part[here, :] + other_part[here, :]
        if rows > 0:
            sums = jnp.concatenate([sums, jnp.zeros((16 - rows, 128), F32)], axis=0)
        high = sums.astype(BF)
        out[at, width : width + 128] = high
        out[at, width + 128 : width + 256] = (sums - high.astype(F32)).astype(BF)


def sds(*shape, dtype=F32):
    return jax.ShapeDtypeStruct(shape, dtype)


def shifted(value, steps):
    n = 64
    first, last = max(0, -steps), min(n, n - steps)
    return lax.ppermute(value, CTX, [(i, i + steps) for i in range(first, last)])


def swapped(value, axis):
    return lax.ppermute(value, axis, [(0, 1), (1, 0)])


def along_y(value, steps):
    pairs = []
    for y in range(4):
        to = (y + steps) % 4
        pairs.append((y % 2 * 2 + y // 2, to % 2 * 2 + to // 2))
    return lax.ppermute(value, ("yl", "yh"), pairs)


def turned_dot(rows, tokens):
    return lax.dot_general(rows, tokens, (((1,), (1,)), ((), ())), preferred_element_type=F32)


def rounded_dot(rows, columns):
    return jnp.dot(rows, columns, preferred_element_type=F32).astype(BF)


def shards(query_proj, key_proj, value_proj, grad_out, out_weight, short_taps, residues, decay_rate):
    q, k, v, go = query_proj[0], key_proj[0], value_proj[0], grad_out[0]
    core, yl, yh = lax.axis_index("core"), lax.axis_index("yl"), lax.axis_index("yh")
    tail = jnp.stack([q[T - 8 :], k[T - 8 :], v[T - 8 :]])
    behind = shifted(tail, 1).astype(F32).reshape(3 * PAD, 128)

    rate = decay_rate.T.reshape(M * 8, 128)
    factor = jnp.exp(-rate)
    norm = jnp.sqrt(-jnp.expm1(-2.0 * rate))
    coef = residues.T.reshape(M * 8, 128) * norm
    taps = jnp.transpose(short_taps, (0, 2, 1)).reshape(21 * 8, 128)
    place = lax.axis_index(CTX)
    span = jnp.exp(-T * lax.dynamic_slice(rate, (2 * place, 0), (2, 128)))

    xs, ys, ends = call(
        shape_kernel, [sds(3 * XR, 128), sds(3 * ROWS, 128), sds(M * 8, 128)], (q, k, v, behind, taps, factor)
    )
    near = lax.all_to_all(jnp.broadcast_to(out_weight[:, :WA], (16, 16, WA)), XZ, 0, 0)
    late = out_weight[:, WA:]
    late = jnp.stack([late, swapped(late, "yl")])
    near, ends = lax.optimization_barrier((near, ends))
    far_low, far_high = along_y(near[:8], 1), along_y(near[8:], -1)
    late = lax.all_to_all(jnp.broadcast_to(late, (16, 2, 16, D - WA)), XZ, 0, 0).reshape(512, D - WA)
    go_theirs = swapped(go, "core")
    go_both = jnp.concatenate([go, go_theirs], axis=0)

    early, rest = go_both[:, :WA], go_both[:, WA:]
    product = [turned_dot(part.reshape(-1, WA), early) for part in (near, far_low, far_high)]
    late, *product = lax.optimization_barrier((late, *product))
    last = turned_dot(late, rest).reshape(16, 2, 16, 2 * T)
    up_both = jnp.concatenate(product, axis=0) + jnp.swapaxes(last, 0, 1).reshape(512, 2 * T)
    up_mine, up_theirs = up_both[:, :T], swapped(up_both[:, T:], "core")
    up, packed = pl.pallas_call(
        back_kernel,
        out_shape=[sds(ROWS, 128), sds(256, 128)],
        in_specs=[pl.BlockSpec(memory_space=pltpu.SMEM)] + [VMEM] * 5,
        out_specs=[VMEM] * 2,
        scratch_shapes=[pltpu.VMEM((M * 8, 128), F32)],
        compiler_params=pltpu.CompilerParams(vmem_limit_bytes=16 * 1024 * 1024),
        cost_estimate=pl.CostEstimate(flops=10_000_000, bytes_accessed=4_000_000, transcendentals=0),
    )(jnp.stack([core, yl]), up_mine, up_theirs, ys, ends, factor)
    head = jnp.concatenate([up[:PAD], ys[:PAD], ys[ROWS : ROWS + PAD], ys[2 * ROWS : 2 * ROWS + PAD]], axis=0)
    ahead = shifted(head, -1)
    blocks = lax.all_to_all(packed.reshape(64, 4, 128), CTX, 0, 0).reshape(256, 128)
    blocks, ahead = lax.optimization_barrier((blocks, ahead))
    (scanned,) = call(scan_kernel, [sds(256, 128)], (blocks, span))
    carries = lax.all_to_all(scanned.reshape(64, 4, 128), CTX, 0, 0).reshape(256, 128)
    filt, gated_t, final = call(
        fore_kernel,
        [sds(ROWS, 128), sds(2, 512, T, dtype=BF), sds(M * 8, 128)],
        (ys, factor, coef, carries),
        [pltpu.VMEM((ROWS, 128), F32)],
    )
    gated_theirs = swapped(lax.dynamic_index_in_dim(gated_t, 1 - core, 0, keepdims=False), "core")
    gated_mine = lax.dynamic_index_in_dim(gated_t, core, 0, keepdims=False)
    gated = jnp.concatenate([gated_mine, gated_theirs], axis=1).reshape(2, 256, 2 * T)
    ours = lax.dynamic_index_in_dim(gated, yl, 0, keepdims=False)
    others = lax.dynamic_index_in_dim(gated, 1 - yl, 0, keepdims=False)
    part_a = GA // 2
    here = lax.dynamic_slice(go_both, (0, part_a * yh), (2 * T, part_a))
    there = lax.dynamic_slice(go_both, (0, part_a * (1 - yh)), (2 * T, part_a))
    parts = [rounded_dot(ours, there), rounded_dot(others, here), rounded_dot(others, there)]
    got = [
        lax.ppermute(parts[0], ("yl", "yh"), [(0, 1), (1, 0), (2, 3), (3, 2)]),
        lax.ppermute(parts[1], ("yl", "yh"), [(0, 2), (2, 0), (1, 3), (3, 1)]),
        lax.ppermute(parts[2], ("yl", "yh"), [(0, 3), (3, 0), (1, 2), (2, 1)]),
    ]
    spread = rounded_dot(jnp.swapaxes(gated.reshape(2, 16, 16, 2 * T), 0, 1).reshape(512, 2 * T), go_both[:, GA:])
    spread = lax.all_to_all(spread.reshape(16, 2, 16, D - GA), XZ, 0, 0)
    first = jnp.dot(ours, here, preferred_element_type=F32)
    oq, ok, ov, sums = call(
        last_kernel,
        [sds(T, C, dtype=BF)] * 3 + [sds(304, 128)],
        (up, filt, ys, xs, ahead, final, carries, factor, coef, jnp.exp(rate), norm, taps),
        [pltpu.VMEM((3 * XR, 128), F32), pltpu.VMEM((ROWS, 128), F32), pltpu.VMEM((M * 8, 128), F32)],
        flops=LAST,
    )
    halves = sums.reshape(2, HALF, 128)
    part = lax.dynamic_index_in_dim(halves, core, 0, keepdims=False)
    other_part = swapped(lax.dynamic_index_in_dim(halves, 1 - core, 0, keepdims=False), "core")
    (joined,) = call(join_kernel, [sds(256, part_a + 256, dtype=BF)], (first, *got, part, other_part))
    joined, spread = lax.optimization_barrier((joined, spread))
    joined = lax.all_to_all(joined.reshape(16, 16, part_a + 256), XZ, 0, 0)
    spread = jnp.sum(spread.astype(F32), axis=0).astype(BF)
    near = lax.dynamic_index_in_dim(spread, yl, 0, keepdims=False)
    far = lax.dynamic_index_in_dim(spread, 1 - yl, 0, keepdims=False)
    levels = [
        swapped(near, "yh"),
        lax.ppermute(far, ("yl", "yh"), [(0, 2), (2, 0), (1, 3), (3, 1)]),
        lax.ppermute(far, ("yl", "yh"), [(0, 3), (3, 0), (1, 2), (2, 1)]),
    ]
    joined, *levels = lax.optimization_barrier((joined, *levels))
    joined = jnp.sum(joined.astype(F32), axis=0)
    first = joined[:, :part_a]
    first_other = swapped(first, "yh")
    part = joined[:, part_a : part_a + 128] + joined[:, part_a + 128 :]
    part = part[:SHARE].reshape(SHARE // 2, 2, 128)
    part = lax.all_to_all(jnp.broadcast_to(part, (64, SHARE // 2, 2, 128)), ("yl", "yh", "x", "z"), 0, 0)
    part = jnp.sum(part.reshape(4, 16 * SHARE, 128)[:, :HALF], axis=0)
    rest = swapped(part, "core")
    level = (near.astype(F32) + levels[0].astype(F32)) + (levels[1].astype(F32) + levels[2].astype(F32))
    weight_grad = jnp.concatenate(
        [jnp.where(yh == 0, first, first_other), jnp.where(yh == 0, first_other, first), level], axis=1
    )
    sums = jnp.where(core == 0, jnp.concatenate([part, rest], axis=0), jnp.concatenate([rest, part], axis=0))
    taps_grad = jnp.transpose(sums[: 21 * 8].reshape(3, 7, C), (0, 2, 1))
    residue_grad = sums[21 * 8 : 37 * 8].reshape(M, C).T
    return (oq[None], ok[None], ov[None], weight_grad, taps_grad, residue_grad)


def solution(mesh):
    grid = Mesh(mesh.devices.reshape(2, 4, 4, 2, 2), ("yl", "x", "z", "core", "yh"))
    stream = P("yh", CTX, None)
    return jax.shard_map(
        shards,
        mesh=grid,
        in_specs=(stream, stream, stream, stream, P(CTX, None), P(), P(), P()),
        out_specs=(stream, stream, stream, P(CTX, None), P(), P()),
        check_vma=False,
    )
```

```python
import jax
import jax.numpy as jnp
from jax import lax
from jax.experimental import pallas as pl
from jax.experimental.pallas import tpu as pltpu
from jax.sharding import Mesh, PartitionSpec as P

BF = jnp.bfloat16
F32 = jnp.float32
T = 128
C = 1024
D = 4096
M = 16
PAD = 64
ROWS = 8 * T
XR = PAD + ROWS
CTX = ("yl", "x", "z", "core")
GRP = ("yl", "x", "z")
XZ = ("x", "z")
WA = 2688
LAST = 7_000_000_000
HALF = 152
SHARE = 10
GA = 2048

VMEM = pl.BlockSpec(memory_space=pltpu.VMEM)


def call(body, outs, ins, scratch=(), flops=10_000_000):
    return pl.pallas_call(
        body,
        out_shape=outs,
        in_specs=[VMEM] * len(ins),
        out_specs=[VMEM] * len(outs),
        scratch_shapes=list(scratch),
        compiler_params=pltpu.CompilerParams(vmem_limit_bytes=16 * 1024 * 1024),
        cost_estimate=pl.CostEstimate(flops=flops, bytes_accessed=4_000_000, transcendentals=0),
    )(*ins)


def row(ref, at):
    return ref[pl.ds(pl.multiple_of(at, 8), 8), :]


def put(ref, at, value):
    ref[pl.ds(pl.multiple_of(at, 8), 8), :] = value


def shape_kernel(q, k, v, halo, taps, factor, xs, ys, ends):
    for i, src in enumerate((q, k, v)):
        base = i * XR
        xs[base : base + PAD, :] = halo[i * PAD : (i + 1) * PAD, :]
        for g in range(T // 16):
            for s in range(8):
                val = src[16 * g : 16 * g + 16, 128 * s : 128 * s + 128].astype(F32)
                xs[pl.ds(base + PAD + 128 * g + s, 16, stride=8), :] = val
    for i in range(3):
        tap = [taps[(i * 7 + j) * 8 : (i * 7 + j) * 8 + 8, :] for j in range(7)]

        def body(b, _):
            at = i * XR + PAD + b * 64
            win = [row(xs, at + 8 * d) for d in range(-6, 8)]
            for t in range(8):
                acc = tap[0] * win[t + 6]
                for j in range(1, 7):
                    acc = acc + tap[j] * win[t + 6 - j]
                put(ys, i * ROWS + b * 64 + 8 * t, acc)
            return 0

        lax.fori_loop(0, T // 8, body, 0)
    fac = [factor[8 * m : 8 * m + 8, :] for m in range(M)]

    def step(b, state):
        for u in range(8):
            at = b * 64 + u * 8
            mixed = row(ys, ROWS + at) * row(ys, 2 * ROWS + at)
            state = tuple(f * x + mixed for f, x in zip(fac, state))
        return state

    state = lax.fori_loop(0, T // 8, step, (jnp.zeros((8, 128), F32),) * M)
    for m in range(M):
        ends[8 * m : 8 * m + 8, :] = state[m]


def tree(terms):
    while len(terms) > 1:
        terms = [a + b for a, b in zip(terms[::2], terms[1::2])]
    return terms[0]


def back_kernel(core, up_mine, up_theirs, ys, ends, factor, up, packed, scr):
    zero = core[0] == 0
    for s in range(8):
        half = jnp.where(core[1] == s // 4, 0, 256)
        blocks = []
        for n in range(4):
            at = pl.ds(pl.multiple_of(half + 64 * (s % 4) + 16 * n, 16), 16)
            one, two = up_mine[at, :], up_theirs[at, :]
            blocks += [jnp.where(zero, one, two), jnp.where(zero, two, one)]
        up[pl.ds(s, T, stride=8), :] = jnp.concatenate(blocks, axis=0).T
    fac = [factor[8 * m : 8 * m + 8, :] for m in range(M)]

    def step(b, state):
        for u in range(8):
            at = ROWS - 8 - b * 64 - u * 8
            grad = row(up, at) * row(ys, at)
            state = tuple(f * x + grad for f, x in zip(fac, state))
        return state

    state = lax.fori_loop(0, T // 8, step, (jnp.zeros((8, 128), F32),) * M)
    for m in range(M):
        scr[8 * m : 8 * m + 8, :] = state[m]
    for n in range(2):
        packed[pl.ds(n, 64, stride=4), :] = ends[pl.ds(n, 64, stride=2), :]
        packed[pl.ds(2 + n, 64, stride=4), :] = scr[pl.ds(n, 64, stride=2), :]


def scan_kernel(parts, span, out):
    decay = span[0:2, :]
    state = jnp.zeros((2, 128), F32)
    for b in range(64):
        out[4 * b : 4 * b + 2, :] = state
        state = decay * state + parts[4 * b : 4 * b + 2, :]
    state = jnp.zeros((2, 128), F32)
    for b in range(63, -1, -1):
        out[4 * b + 2 : 4 * b + 4, :] = state
        state = decay * state + parts[4 * b + 2 : 4 * b + 4, :]


def fore_kernel(ys, factor, coef, carries, filt, gated_t, final, scr):
    for n in range(2):
        final[pl.ds(n, 64, stride=2), :] = carries[pl.ds(n, 64, stride=4), :]
    state = tuple(final[8 * m : 8 * m + 8, :] for m in range(M))

    def step(b, state):
        for u in range(4):
            at = b * 32 + u * 8
            mixed = row(ys, ROWS + at) * row(ys, 2 * ROWS + at)
            state = tuple(factor[8 * m : 8 * m + 8, :] * state[m] + mixed for m in range(M))
            value = tree([coef[8 * m : 8 * m + 8, :] * state[m] for m in range(M)])
            put(filt, at, value)
            put(scr, at, value * row(ys, at))
        return state

    state = lax.fori_loop(0, T // 4, step, state)
    for m in range(M):
        final[8 * m : 8 * m + 8, :] = state[m]
    for s in range(8):
        turned = scr[pl.ds(s, T, stride=8), :].T.astype(BF)
        for n in range(8):
            at = 64 * s + 16 * (n // 2)
            gated_t[n % 2, at : at + 16, :] = turned[16 * n : 16 * n + 16, :]


def last_kernel(
    up, filt, ys, xs, halo, final, carries, factor, coef, inverse, norm, taps, oq, ok, ov, sums, gs, res, outgoing
):
    for n in range(2):
        outgoing[pl.ds(n, 64, stride=2), :] = carries[pl.ds(2 + n, 64, stride=4), :]
    sums[37 * 8 :, :] = jnp.zeros((8, 128), F32)
    adj = [outgoing[8 * m : 8 * m + 8, :] for m in range(M)]
    state = [final[8 * m : 8 * m + 8, :] for m in range(M)]
    for n in range(6):
        nup, nq, nk, nv = (halo[i * PAD + 8 * n : i * PAD + 8 * n + 8, :] for i in range(4))
        mixed = nk * nv
        state = [factor[8 * m : 8 * m + 8, :] * state[m] + mixed for m in range(M)]
        value = tree([coef[8 * m : 8 * m + 8, :] * state[m] for m in range(M)])
        mix = tree([coef[8 * m : 8 * m + 8, :] * adj[m] for m in range(M)])
        put(gs, ROWS + 8 * n, nup * value)
        put(gs, XR + ROWS + 8 * n, mix * nv)
        put(gs, 2 * XR + ROWS + 8 * n, mix * nk)
        if n < 5:
            first = nup * nq
            adj = [(adj[m] - first) * inverse[8 * m : 8 * m + 8, :] for m in range(M)]
    for n in range(6, 8):
        for i in range(3):
            put(gs, i * XR + ROWS + 8 * n, jnp.zeros((8, 128), F32))
    half = M // 2
    for part in range(2):
        ms = range(part * half, (part + 1) * half)
        adj = tuple(outgoing[8 * m : 8 * m + 8, :] for m in ms)
        total = (jnp.zeros((8, 128), F32),) * half

        def step(b, carry):
            adj, total = carry
            for u in range(4):
                at = ROWS - 8 - b * 32 - u * 8
                grad = row(up, at) * row(ys, at)
                ks, vs = row(ys, ROWS + at), row(ys, 2 * ROWS + at)
                mixed = ks * vs
                adj = tuple(factor[8 * m : 8 * m + 8, :] * a + grad for m, a in zip(ms, adj))
                total = tuple(t + mixed * a for t, a in zip(total, adj))
                mix = tree([coef[8 * m : 8 * m + 8, :] * a for m, a in zip(ms, adj)])
                if part == 0:
                    put(res, at, mix)
                else:
                    mix = mix + row(res, at)
                    put(gs, at, row(up, at) * row(filt, at))
                    put(gs, XR + at, mix * vs)
                    put(gs, 2 * XR + at, mix * ks)
            return adj, total

        adj, total = lax.fori_loop(0, T // 4, step, (adj, total))
        for m, t in zip(ms, total):
            sums[21 * 8 + 8 * m : 21 * 8 + 8 * m + 8, :] = t * norm[8 * m : 8 * m + 8, :]
    for i, out in enumerate((oq, ok, ov)):
        tap = [taps[(i * 7 + j) * 8 : (i * 7 + j) * 8 + 8, :] for j in range(7)]

        def body(b, acc):
            at = i * XR + b * 64
            win = [row(gs, at + 8 * d) for d in range(14)]
            field = [row(xs, at + PAD + 8 * d) for d in range(-6, 8)]
            acc = list(acc)
            for t in range(8):
                value = tap[0] * win[t]
                for j in range(1, 7):
                    value = value + tap[j] * win[t + j]
                put(res, b * 64 + 8 * t, value)
                for j in range(7):
                    acc[j] = acc[j] + win[t] * field[t + 6 - j]
            return tuple(acc)

        acc = lax.fori_loop(0, T // 8, body, (jnp.zeros((8, 128), F32),) * 7)
        for j in range(7):
            sums[(i * 7 + j) * 8 : (i * 7 + j) * 8 + 8, :] = acc[j]
        for g in range(T // 16):
            for s in range(8):
                val = res[pl.ds(128 * g + s, 16, stride=8), :]
                out[16 * g : 16 * g + 16, 128 * s : 128 * s + 128] = val.astype(BF)


def join_kernel(own, one, two, three, part, other_part, out):
    width = own.shape[1]
    for d in range(16):
        at = slice(16 * d, 16 * d + 16)
        value = own[at, :] + one[at, :].astype(F32) + two[at, :].astype(F32) + three[at, :].astype(F32)
        out[at, 0:width] = value.astype(BF)
        here = slice(SHARE * d, min(SHARE * d + SHARE, HALF))
        rows = max(0, here.stop - here.start)
        sums = jnp.zeros((16, 128), F32)
        if rows > 0:
            sums = part[here, :] + other_part[here, :]
        if rows > 0:
            sums = jnp.concatenate([sums, jnp.zeros((16 - rows, 128), F32)], axis=0)
        high = sums.astype(BF)
        out[at, width : width + 128] = high
        out[at, width + 128 : width + 256] = (sums - high.astype(F32)).astype(BF)


def sds(*shape, dtype=F32):
    return jax.ShapeDtypeStruct(shape, dtype)


def shifted(value, steps):
    n = 64
    first, last = max(0, -steps), min(n, n - steps)
    return lax.ppermute(value, CTX, [(i, i + steps) for i in range(first, last)])


def swapped(value, axis):
    return lax.ppermute(value, axis, [(0, 1), (1, 0)])


def along_y(value, steps):
    pairs = []
    for y in range(4):
        to = (y + steps) % 4
        pairs.append((y % 2 * 2 + y // 2, to % 2 * 2 + to // 2))
    return lax.ppermute(value, ("yl", "yh"), pairs)


def turned_dot(rows, tokens):
    return lax.dot_general(rows, tokens, (((1,), (1,)), ((), ())), preferred_element_type=F32)


def rounded_dot(rows, columns):
    return jnp.dot(rows, columns, preferred_element_type=F32).astype(BF)


def shards(query_proj, key_proj, value_proj, grad_out, out_weight, short_taps, residues, decay_rate):
    q, k, v, go = query_proj[0], key_proj[0], value_proj[0], grad_out[0]
    core, yl, yh = lax.axis_index("core"), lax.axis_index("yl"), lax.axis_index("yh")
    tail = jnp.stack([q[T - 8 :], k[T - 8 :], v[T - 8 :]])
    behind = shifted(tail, 1).astype(F32).reshape(3 * PAD, 128)

    rate = decay_rate.T.reshape(M * 8, 128)
    factor = jnp.exp(-rate)
    norm = jnp.sqrt(-jnp.expm1(-2.0 * rate))
    coef = residues.T.reshape(M * 8, 128) * norm
    taps = jnp.transpose(short_taps, (0, 2, 1)).reshape(21 * 8, 128)
    place = lax.axis_index(CTX)
    span = jnp.exp(-T * lax.dynamic_slice(rate, (2 * place, 0), (2, 128)))

    xs, ys, ends = call(
        shape_kernel, [sds(3 * XR, 128), sds(3 * ROWS, 128), sds(M * 8, 128)], (q, k, v, behind, taps, factor)
    )
    near = lax.all_to_all(jnp.broadcast_to(out_weight[:, :WA], (16, 16, WA)), XZ, 0, 0)
    late = out_weight[:, WA:]
    late = jnp.stack([late, swapped(late, "yl")])
    near, ends = lax.optimization_barrier((near, ends))
    far_low, far_high = along_y(near[:8], 1), along_y(near[8:], -1)
    late = lax.all_to_all(jnp.broadcast_to(late, (16, 2, 16, D - WA)), XZ, 0, 0).reshape(512, D - WA)
    go_theirs = swapped(go, "core")
    go_both = jnp.concatenate([go, go_theirs], axis=0)

    early, rest = go_both[:, :WA], go_both[:, WA:]
    product = [turned_dot(part.reshape(-1, WA), early) for part in (near, far_low, far_high)]
    late, *product = lax.optimization_barrier((late, *product))
    last = turned_dot(late, rest).reshape(16, 2, 16, 2 * T)
    up_both = jnp.concatenate(product, axis=0) + jnp.swapaxes(last, 0, 1).reshape(512, 2 * T)
    up_mine, up_theirs = up_both[:, :T], swapped(up_both[:, T:], "core")
    up, packed = pl.pallas_call(
        back_kernel,
        out_shape=[sds(ROWS, 128), sds(256, 128)],
        in_specs=[pl.BlockSpec(memory_space=pltpu.SMEM)] + [VMEM] * 5,
        out_specs=[VMEM] * 2,
        scratch_shapes=[pltpu.VMEM((M * 8, 128), F32)],
        compiler_params=pltpu.CompilerParams(vmem_limit_bytes=16 * 1024 * 1024),
        cost_estimate=pl.CostEstimate(flops=10_000_000, bytes_accessed=4_000_000, transcendentals=0),
    )(jnp.stack([core, yl]), up_mine, up_theirs, ys, ends, factor)
    head = jnp.concatenate([up[:PAD], ys[:PAD], ys[ROWS : ROWS + PAD], ys[2 * ROWS : 2 * ROWS + PAD]], axis=0)
    ahead = shifted(head, -1)
    blocks = lax.all_to_all(packed.reshape(64, 4, 128), CTX, 0, 0).reshape(256, 128)
    (scanned,) = call(scan_kernel, [sds(256, 128)], (blocks, span))
    carries = lax.all_to_all(scanned.reshape(64, 4, 128), CTX, 0, 0).reshape(256, 128)
    carries, ahead = lax.optimization_barrier((carries, ahead))
    filt, gated_t, final = call(
        fore_kernel,
        [sds(ROWS, 128), sds(2, 512, T, dtype=BF), sds(M * 8, 128)],
        (ys, factor, coef, carries),
        [pltpu.VMEM((ROWS, 128), F32)],
    )
    gated_theirs = swapped(lax.dynamic_index_in_dim(gated_t, 1 - core, 0, keepdims=False), "core")
    gated_mine = lax.dynamic_index_in_dim(gated_t, core, 0, keepdims=False)
    gated = jnp.concatenate([gated_mine, gated_theirs], axis=1).reshape(2, 256, 2 * T)
    ours = lax.dynamic_index_in_dim(gated, yl, 0, keepdims=False)
    others = lax.dynamic_index_in_dim(gated, 1 - yl, 0, keepdims=False)
    part_a = GA // 2
    here = lax.dynamic_slice(go_both, (0, part_a * yh), (2 * T, part_a))
    there = lax.dynamic_slice(go_both, (0, part_a * (1 - yh)), (2 * T, part_a))
    parts = [rounded_dot(ours, there), rounded_dot(others, here), rounded_dot(others, there)]
    got = [
        lax.ppermute(parts[0], ("yl", "yh"), [(0, 1), (1, 0), (2, 3), (3, 2)]),
        lax.ppermute(parts[1], ("yl", "yh"), [(0, 2), (2, 0), (1, 3), (3, 1)]),
        lax.ppermute(parts[2], ("yl", "yh"), [(0, 3), (3, 0), (1, 2), (2, 1)]),
    ]
    spread = rounded_dot(jnp.swapaxes(gated.reshape(2, 16, 16, 2 * T), 0, 1).reshape(512, 2 * T), go_both[:, GA:])
    spread = lax.all_to_all(spread.reshape(16, 2, 16, D - GA), XZ, 0, 0)
    first = jnp.dot(ours, here, preferred_element_type=F32)
    oq, ok, ov, sums = call(
        last_kernel,
        [sds(T, C, dtype=BF)] * 3 + [sds(304, 128)],
        (up, filt, ys, xs, ahead, final, carries, factor, coef, jnp.exp(rate), norm, taps),
        [pltpu.VMEM((3 * XR, 128), F32), pltpu.VMEM((ROWS, 128), F32), pltpu.VMEM((M * 8, 128), F32)],
        flops=LAST,
    )
    halves = sums.reshape(2, HALF, 128)
    part = lax.dynamic_index_in_dim(halves, core, 0, keepdims=False)
    other_part = swapped(lax.dynamic_index_in_dim(halves, 1 - core, 0, keepdims=False), "core")
    (joined,) = call(join_kernel, [sds(256, part_a + 256, dtype=BF)], (first, *got, part, other_part))
    joined, spread = lax.optimization_barrier((joined, spread))
    joined = lax.all_to_all(joined.reshape(16, 16, part_a + 256), XZ, 0, 0)
    spread = jnp.sum(spread.astype(F32), axis=0).astype(BF)
    near = lax.dynamic_index_in_dim(spread, yl, 0, keepdims=False)
    far = lax.dynamic_index_in_dim(spread, 1 - yl, 0, keepdims=False)
    levels = [
        swapped(near, "yh"),
        lax.ppermute(far, ("yl", "yh"), [(0, 2), (2, 0), (1, 3), (3, 1)]),
        lax.ppermute(far, ("yl", "yh"), [(0, 3), (3, 0), (1, 2), (2, 1)]),
    ]
    joined, *levels = lax.optimization_barrier((joined, *levels))
    joined = jnp.sum(joined.astype(F32), axis=0)
    first = joined[:, :part_a]
    first_other = swapped(first, "yh")
    part = joined[:, part_a : part_a + 128] + joined[:, part_a + 128 :]
    part = part[:SHARE].reshape(SHARE // 2, 2, 128)
    part = lax.all_to_all(jnp.broadcast_to(part, (64, SHARE // 2, 2, 128)), ("yl", "yh", "x", "z"), 0, 0)
    part = jnp.sum(part.reshape(4, 16 * SHARE, 128)[:, :HALF], axis=0)
    rest = swapped(part, "core")
    level = (near.astype(F32) + levels[0].astype(F32)) + (levels[1].astype(F32) + levels[2].astype(F32))
    weight_grad = jnp.concatenate(
        [jnp.where(yh == 0, first, first_other), jnp.where(yh == 0, first_other, first), level], axis=1
    )
    sums = jnp.where(core == 0, jnp.concatenate([part, rest], axis=0), jnp.concatenate([rest, part], axis=0))
    taps_grad = jnp.transpose(sums[: 21 * 8].reshape(3, 7, C), (0, 2, 1))
    residue_grad = sums[21 * 8 : 37 * 8].reshape(M, C).T
    return (oq[None], ok[None], ov[None], weight_grad, taps_grad, residue_grad)


def solution(mesh):
    grid = Mesh(mesh.devices.reshape(2, 4, 4, 2, 2), ("yl", "x", "z", "core", "yh"))
    stream = P("yh", CTX, None)
    return jax.shard_map(
        shards,
        mesh=grid,
        in_specs=(stream, stream, stream, stream, P(CTX, None), P(), P(), P()),
        out_specs=(stream, stream, stream, P(CTX, None), P(), P()),
        check_vma=False,
    )
```
